128 devices in a mesh: dp: 16 (over y, z_hi, core), row: 4 (over x), col: 2 (over z_lo).
Axes of the slice: x: 4, y: 4, z: 4 (z_hi: 2, z_lo: 2; z = z_hi * 2 + z_lo), core: 2. Of those that a mesh axis runs over, the one named last changes fastest.
Arguments:
- inputs: bfloat16 [16, 1024, 1152], P('dp', 'row', 'col'), may hold values from -6 to 6
- w_query: bfloat16 [1152, 1024], P('col', 'row'), may hold values from -0.1875 to 0.1875
- w_key: bfloat16 [1152, 256], P('col'), may hold values from -0.1875 to 0.1875
- w_value: bfloat16 [1152, 256], P('col'), may hold values from -0.1875 to 0.1875
- attention_output_weight: bfloat16 [1024, 1152], P('row', 'col'), may hold values from -0.1875 to 0.1875
- w_gate: bfloat16 [1152, 6912], P('col', 'row'), may hold values from -0.1875 to 0.1875
- w_up: bfloat16 [1152, 6912], P('col', 'row'), may hold values from -0.1875 to 0.1875
- down_weight: bfloat16 [6912, 1152], P('row', 'col'), may hold values from -0.078125 to 0.078125
- g_in: float32 [1152], P('col'), may hold values from 0.25 to 1.75
- g_query: float32 [256], replicated, may hold values from 0.25 to 1.75
- g_key: float32 [256], replicated, may hold values from 0.25 to 1.75
- g_post_attn: float32 [1152], P('col'), may hold values from 0.25 to 1.75
- g_pre_ffn: float32 [1152], P('col'), may hold values from 0.25 to 1.75
- g_post_ffn: float32 [1152], P('col'), may hold values from 0.25 to 1.75
- cotangent: bfloat16 [16, 1024, 1152], P('dp', 'row', 'col'), may hold values from -6 to 6
Outputs:
- block_out: bfloat16 [16, 1024, 1152], P('dp', 'row', 'col')
- grad_inputs: bfloat16 [16, 1024, 1152], P('dp', 'row', 'col')
- grad_w_query: float32 [1152, 1024], P('col', 'row')
- grad_w_key: float32 [1152, 256], P('col')
- grad_w_value: float32 [1152, 256], P('col')
- grad_w_out: float32 [1024, 1152], P('row', 'col')
- grad_w_gate: float32 [1152, 6912], P('col', 'row')
- grad_w_up: float32 [1152, 6912], P('col', 'row')
- grad_w_down: float32 [6912, 1152], P('row', 'col')
- grad_g_in: float32 [1152], P('col')
- grad_g_query: float32 [256], replicated
- grad_g_key: float32 [256], replicated
- grad_g_post_attn: float32 [1152], P('col')
- grad_g_pre_ffn: float32 [1152], P('col')
- grad_g_post_ffn: float32 [1152], P('col')
The draws below stay inside these ranges and needn't reach their ends.
All inputs are finite; a program needn't handle non-finite values.
Results may differ from the reference program's by a relative error of at most 0.025.
Values may be sent and summed in bfloat16 or wider, within the bound.
No kernel may reach another device: no remote copies, remote signals or barrier semaphores. Data moves between devices by JAX's collectives and lax.ppermute only.
A program may use at most 128 MiB of HBM per device.

```python
import jax
import jax.numpy as jnp
from jax import lax

D = 1152
HEADS = 4
HEAD = 256
FF = 6912
WINDOW = 512
LEN = 1024
SEQS = 16


def draw_inputs(key, part):
    key = jax.random.fold_in(key, 11)
    feature = jnp.arange(D, dtype=jnp.float32) / D
    base = jnp.clip(jax.random.normal(key, (SEQS, LEN, D), jnp.float32), -4.0, 4.0)
    ramp = 0.5 + feature
    return (base * ramp[None, None, :]).astype(jnp.bfloat16)


def draw_cotangent(key, part):
    key = jax.random.fold_in(key, 23)
    ramp = (0.5 + jnp.arange(SEQS, dtype=jnp.float32) / SEQS)[:, None, None]
    base = jnp.clip(jax.random.normal(key, (SEQS, LEN, D), jnp.float32), -4.0, 4.0)
    return (base * ramp).astype(jnp.bfloat16)


def block_scale(key, extent, pieces, least, high):
    def one(dim, parts):
        steps = jax.random.uniform(jax.random.fold_in(jax.random.fold_in(key, 6), dim), (parts,), jnp.float32, least / len(pieces), high / len(pieces))
        return jnp.repeat(jnp.exp(steps), extent[dim] // parts).reshape((-1,) + (1,) * (len(extent) - dim - 1))

    factor_of = one(*pieces[0])
    for cut in pieces[1:]:
        factor_of = factor_of * one(*cut)
    return factor_of


def normal_values(key, extent, spread, most, cuts=(), held_as=jnp.bfloat16):
    drawn = spread * jax.random.normal(key, extent, jnp.float32)
    if cuts:
        drawn = drawn * block_scale(key, extent, cuts, -0.22, 0.18)
    return jnp.clip(drawn, -most, most).astype(held_as)


def setup_inputs(seed: int = 0) -> dict:
    key_list = jax.random.split(jax.random.key(seed), 16)
    return {
        "inputs": draw_inputs(jax.random.fold_in(key_list[15], 71), 0),
        "w_query": normal_values(key_list[1], (D, HEADS * HEAD), D ** -0.5, 0.1875, ((0, 2), (1, 4))),
        "w_key": normal_values(key_list[2], (D, HEAD), D ** -0.5, 0.1875, ((0, 2),)),
        "w_value": normal_values(key_list[3], (D, HEAD), D ** -0.5, 0.1875, ((0, 2),)),
        "attention_output_weight": normal_values(key_list[4], (HEADS * HEAD, D), (HEADS * HEAD) ** -0.5, 0.1875, ((0, 4), (1, 2))),
        "w_gate": normal_values(key_list[5], (D, FF), D ** -0.5, 0.1875, ((0, 2), (1, 4))),
        "w_up": normal_values(key_list[6], (D, FF), D ** -0.5, 0.1875, ((0, 2), (1, 4))),
        "down_weight": normal_values(key_list[7], (FF, D), FF ** -0.5, 0.078125, ((0, 4), (1, 2))),
        "g_in": jnp.clip(1.0 + 0.15 * jax.random.normal(key_list[8], (D,), jnp.float32), 0.25, 1.75),
        "g_query": jnp.clip(1.0 + 0.15 * jax.random.normal(key_list[9], (HEAD,), jnp.float32), 0.25, 1.75),
        "g_key": jnp.clip(1.0 + 0.15 * jax.random.normal(key_list[10], (HEAD,), jnp.float32), 0.25, 1.75),
        "g_post_attn": jnp.clip(1.0 + 0.15 * jax.random.normal(key_list[11], (D,), jnp.float32), 0.25, 1.75),
        "g_pre_ffn": jnp.clip(1.0 + 0.15 * jax.random.normal(key_list[12], (D,), jnp.float32), 0.25, 1.75),
        "g_post_ffn": jnp.clip(1.0 + 0.15 * jax.random.normal(key_list[13], (D,), jnp.float32), 0.25, 1.75),
        "cotangent": draw_cotangent(jax.random.fold_in(key_list[15], 71), 0),
    }


EPSILON = 1e-06
MASKED = -1e+30
ROPE_BASE = 10000.0

@jax.custom_vjp
def low(v):
    return lax.optimization_barrier(v.astype(jnp.bfloat16)).astype(jnp.float32)

@jax.custom_vjp
def low_back(v):
    return v

def low_keep(v):
    return (low(v), None)

def low_pass(kept, grad):
    return (grad,)

def back_keep(v):
    return (v, None)

def back_low(kept, grad):
    return (low(grad),)
low.defvjp(low_keep, low_pass)
low_back.defvjp(back_keep, back_low)

def product(left, right):
    return jnp.dot(left, right, precision=lax.Precision.HIGHEST, preferred_element_type=jnp.float32)

def rms_scale(values, gain_vec):
    return values * lax.rsqrt(lax.optimization_barrier(jnp.mean(values * values, axis=-1, keepdims=True)) + EPSILON) * gain_vec

def rotate(values, position):
    half_size = values.shape[-1] // 2
    exponent = jnp.arange(half_size, dtype=jnp.float32) * (2.0 / values.shape[-1])
    angles = position.astype(jnp.float32)[:, None] * (ROPE_BASE ** (-exponent))[None, :]
    cosine = jnp.cos(angles)
    sine = jnp.sin(angles)
    first = values[..., :half_size]
    second = values[..., half_size:]
    return jnp.concatenate([first * cosine - second * sine, second * cosine + first * sine], axis=-1)

@jax.checkpoint
def attend(query_rot, key_rot, value_low):
    length = query_rot.shape[1]
    position = jnp.arange(length, dtype=jnp.int32)
    offset = position[:, None] - position[None, :]
    allowed = (offset >= 0) & (offset < WINDOW)
    scores = low_back(jnp.einsum('hqd,hkd->hqk', query_rot, key_rot, precision=lax.Precision.HIGHEST))
    attn_probs = jax.nn.softmax(jnp.where(allowed[None], scores, MASKED), axis=-1)
    return jnp.einsum('hqk,hkd->hqd', low(attn_probs), value_low, precision=lax.Precision.HIGHEST)

def block_layer(inputs, w_query, w_key, w_value, attention_output_weight, w_gate, w_up, down_weight, g_in, g_query, g_key, g_post_attn, g_pre_ffn, g_post_ffn):
    length = inputs.shape[0]
    position = jnp.arange(length, dtype=jnp.int32)
    attn_in = low(rms_scale(inputs, g_in))
    query_heads = low_back(product(attn_in, w_query).reshape(length, HEADS, HEAD).transpose(1, 0, 2))
    key_heads = low_back(jnp.broadcast_to(product(attn_in, w_key)[None], (HEADS, length, HEAD)))
    value_heads = low_back(jnp.broadcast_to(product(attn_in, w_value)[None], (HEADS, length, HEAD)))
    query_rot = low(rotate(rms_scale(query_heads, g_query), position) * HEAD ** (-0.5))
    key_rot = low(rotate(rms_scale(key_heads, g_key), position))
    mixed_heads = low(low_back(attend(query_rot, key_rot, low(value_heads))))
    branch = low_back(product(mixed_heads.transpose(1, 0, 2).reshape(length, HEADS * HEAD), attention_output_weight))
    middle = inputs + rms_scale(branch, g_post_attn)
    ffn_in = low(rms_scale(middle, g_pre_ffn))
    gate_proj = low_back(product(ffn_in, w_gate))
    up_proj = low_back(product(ffn_in, w_up))
    hidden = low(jax.nn.gelu(gate_proj, approximate=True) * up_proj)
    down_proj = low_back(product(hidden, down_weight))
    return middle + rms_scale(down_proj, g_post_ffn)

def reference(inputs, w_query, w_key, w_value, attention_output_weight, w_gate, w_up, down_weight, g_in, g_query, g_key, g_post_attn, g_pre_ffn, g_post_ffn, cotangent):
    params = tuple((member.astype(jnp.float32) for member in (w_query, w_key, w_value, attention_output_weight, w_gate, w_up, down_weight, g_in, g_query, g_key, g_post_attn, g_pre_ffn, g_post_ffn)))
    zeros_init = tuple((jnp.zeros(member.shape, jnp.float32) for member in params))

    def per_sequence(running, sequence_pair):
        sequence, upstream = sequence_pair
        result, pull_back = jax.vjp(block_layer, sequence.astype(jnp.float32), *params)
        grads_all = pull_back(upstream.astype(jnp.float32))
        summed = tuple((before + update for before, update in zip(running, grads_all[1:])))
        return (summed, (result.astype(jnp.bfloat16), grads_all[0].astype(jnp.bfloat16)))
    summed, outputs = lax.scan(per_sequence, zeros_init, (inputs, cotangent))
    return (outputs[0], outputs[1], summed[0], summed[1], summed[2], summed[3], summed[4], summed[5], summed[6], summed[7], summed[8], summed[9], summed[10], summed[11], summed[12])
```

```python
import jax
import jax.numpy as jnp
import numpy as np
from jax import lax
from jax.sharding import PartitionSpec as P

WINDOW = 512
EPSILON = 1e-06
MASKED = -1e30
ROPE_BASE = 10000.0
LOW = jnp.bfloat16
WIDE = jnp.float32

Y, HI, CORE, COL, ROW = 4, 2, 2, 2, 4


def device(y, z, core):
    return ((y * HI + z // COL) * CORE + core) * COL + z % COL


def z_route(shift_of):
    return [
        (device(y, z, core), device(y, (z + shift_of(z, core)) % 4, core))
        for y in range(Y)
        for z in range(4)
        for core in range(CORE)
    ]


def dp_route(target):
    return [(i, target(i)) for i in range(Y * HI * CORE)]


def by_z(shift_of):
    route = z_route(shift_of)
    return lambda v: lax.ppermute(v, ("dp", "col"), route)


to_partner = by_z(lambda z, core: 1 if z % 2 == 0 else -1)
to_cross = by_z(lambda z, core: -1 if z % 2 == 0 else 1)
to_opposite = by_z(lambda z, core: 2)
z_ring = by_z(lambda z, core: -1 if core == 0 else 1)


def core_swap(v):
    return lax.ppermute(v, "dp", dp_route(lambda i: i ^ 1))


def y_ring(v):
    step = HI * CORE
    return lax.ppermute(
        v, "dp", dp_route(lambda i: (i + (step if i % 2 == 0 else -step)) % (Y * step))
    )


def y_shift(v, distance):
    step = HI * CORE * distance
    return lax.ppermute(v, "dp", dp_route(lambda i: (i + step) % (Y * HI * CORE)))


def row_shift(v, distance):
    return lax.ppermute(v, "row", [(i, (i + distance) % ROW) for i in range(ROW)])


def row_gather(v):
    return jnp.concatenate([v, row_shift(v, 1), row_shift(v, -1), row_shift(v, 2)], axis=1)


def row_scatter(total):
    share = total.shape[1] // ROW
    own, *others = [total[:, i * share : (i + 1) * share] for i in range(ROW)]
    for part, distance in ((others[2], 2), (others[0], -1), (others[1], 1)):
        own = own + row_shift(part.astype(LOW), distance).astype(WIDE)
    return own


def dot(left, right, dims):
    return lax.dot_general(left, right, (dims, ((), ())), preferred_element_type=WIDE)


def norm(v, gain):
    factor = lax.rsqrt(jnp.sum(v * v, axis=0, keepdims=True) / v.shape[0] + EPSILON)
    return v * factor * gain, factor


def norm_back(v, factor, gain, upstream):
    scaled = upstream * gain
    inner = jnp.sum(scaled * v, axis=0, keepdims=True)
    grad = factor * scaled - v * (factor * factor * factor) * inner / v.shape[0]
    return grad, jnp.sum(upstream * v * factor, axis=1)


def head_map(raw, gain, cosine, sine, scaling):
    normed = (
        raw * lax.rsqrt(jnp.mean(raw * raw, axis=0, keepdims=True) + EPSILON) * gain[:, None]
    )
    half = raw.shape[0] // 2
    first, second = normed[:half], normed[half:]
    turned = jnp.concatenate(
        [first * cosine - second * sine, second * cosine + first * sine], axis=0
    )
    return turned * scaling


def geglu(gate, up):
    return jax.nn.gelu(gate, approximate=True) * up


def rope_tables(length, head_size):
    half = head_size // 2
    exponent = np.arange(half, dtype=np.float32) * np.float32(2.0 / head_size)
    rate = np.float32(ROPE_BASE) ** (-exponent)
    angles = rate[:, None] * np.arange(length, dtype=np.float32)[None, :]
    return np.stack([np.cos(angles), np.sin(angles)]).astype(np.float32)


def pick(v, index, axis):
    return lax.dynamic_index_in_dim(v, index, axis, keepdims=False)


def fetch(own, core):
    half = own.shape[0] // 2
    mine = z_ring(lax.dynamic_slice_in_dim(own, core * half, half, 0))
    return mine


def assemble(own, mine, core):
    theirs = core_swap(mine)
    first = jnp.where(core == 0, mine, theirs)
    second = jnp.where(core == 0, theirs, mine)
    return jnp.concatenate([own, first, second], axis=0)


def add(a, b):
    return (a.astype(WIDE) + b.astype(WIDE)).astype(LOW)


def reduce_weight(grad, place):
    y, hi, core = place
    width = grad.shape[1]
    parts = grad.reshape(COL, CORE, -1, width)
    held = add(pick(parts, core, 1), core_swap(pick(parts, 1 - core, 1)))
    chunks = held.reshape(COL, Y, -1, width)
    way = 1 - 2 * core

    def chunk(steps):
        return pick(chunks, (y - steps * way) % Y, 1)

    total = chunk(1)
    for step in range(Y - 1):
        total = add(y_ring(total), chunk(step + 2))
    halves = total.reshape(COL, -1, HI, width // HI)
    near, far = pick(halves, hi, 2), pick(halves, 1 - hi, 2)
    piece = (
        near[0].astype(WIDE)
        + to_partner(near[1]).astype(WIDE)
        + to_cross(far[1]).astype(WIDE)
        + to_opposite(far[0]).astype(WIDE)
    ).astype(LOW)
    other = to_opposite(piece)
    piece = jnp.where(
        hi == 0,
        jnp.concatenate([piece, other], axis=1),
        jnp.concatenate([other, piece], axis=1),
    )
    ring = [piece]
    for step in range(Y - 1):
        ring.append(y_ring(ring[-1]))
    ring = jnp.stack(ring)
    mine = jnp.concatenate([pick(ring, (way * (y - j)) % Y, 0) for j in range(Y)], axis=0)
    theirs = core_swap(mine)
    return jnp.where(
        core == 0,
        jnp.concatenate([mine, theirs], axis=0),
        jnp.concatenate([theirs, mine], axis=0),
    )


def reduce_gains(gains):
    total = gains + core_swap(gains)
    total = total + y_shift(total, 1) + y_shift(total, 2) + y_shift(total, 3)
    total = total + row_shift(total, 1) + row_shift(total, 2) + row_shift(total, 3)
    total = total + to_opposite(total)
    theirs = to_partner(total)
    return (total + jnp.concatenate([theirs[::-1, :4], theirs[:, 4:]], axis=1))


def local(
    inputs,
    w_query,
    w_key,
    w_value,
    attention_output_weight,
    w_gate,
    w_up,
    down_weight,
    g_in,
    g_query,
    g_key,
    g_post_attn,
    g_pre_ffn,
    g_post_ffn,
    cotangent,
):
    col, row, dp = lax.axis_index("col"), lax.axis_index("row"), lax.axis_index("dp")
    core, hi, y = dp % CORE, (dp // CORE) % HI, dp // (HI * CORE)
    place = (y, hi, core)
    features, share = inputs.shape[2], inputs.shape[1] // COL
    head = g_query.shape[0]
    hidden_share = w_gate.shape[1]
    padding = -hidden_share % 256
    barrier = lax.optimization_barrier

    def spread(v):
        kept = lax.dynamic_slice_in_dim(v, col * share, share, 1)
        given = lax.dynamic_slice_in_dim(v, (1 - col) * share, share, 1)
        return kept, to_partner(given)

    def back_together(v):
        kept, given = v[:features], v[features:]
        theirs = to_partner(given)
        return jnp.where(
            col == 0,
            jnp.concatenate([kept, theirs], axis=1),
            jnp.concatenate([theirs, kept], axis=1),
        )

    gains_own = jnp.stack([g_in, g_post_attn, g_pre_ffn, g_post_ffn])
    gains = jnp.concatenate([gains_own, to_partner(gains_own)], axis=1).T
    gain_in, gain_post_attn, gain_pre_ffn, gain_post_ffn = [gains[:, i : i + 1] for i in range(4)]

    kept, taken = spread(inputs[0].T)
    attn_own = jnp.concatenate([w_query, w_key, w_value, attention_output_weight.T], axis=1)
    attn_own, taken = barrier((attn_own, taken))
    attn_weight = assemble(attn_own, fetch(attn_own, core), core)
    qkv_weight, out_weight = attn_weight[:, : 3 * head], attn_weight[:, 3 * head :]

    pad = lambda w: jnp.pad(w, ((0, 0), (0, padding)))
    ffn_own = jnp.concatenate([pad(w_gate), pad(w_up), pad(down_weight.T)], axis=1)
    wide = hidden_share + padding
    ffn_mine = fetch(barrier((ffn_own, taken))[0], core)

    x = jnp.concatenate([kept, taken], axis=0).astype(WIDE)
    attn_norm, attn_factor = norm(x, gain_in)
    attn_in = row_gather(attn_norm.astype(LOW))
    qkv = dot(qkv_weight, attn_in, ((0,), (0,)))
    raw_query, raw_key, value = qkv[:head], qkv[head : 2 * head], qkv[2 * head :].astype(LOW)

    chunk_rows = [row, (row - 1) % ROW, (row + 1) % ROW, (row + 2) % ROW]
    tables = jnp.asarray(rope_tables(ROW * COL * share, head))
    turns = jnp.concatenate(
        [
            lax.dynamic_slice_in_dim(tables, (r * COL + col) * share, share, 2)
            for r in chunk_rows
        ],
        axis=2,
    )
    cosine, sine = turns[0], turns[1]
    query_rot, query_pull = jax.vjp(
        lambda v, g: head_map(v, g, cosine, sine, head**-0.5), raw_query, g_query
    )
    key_rot, key_pull = jax.vjp(lambda v, g: head_map(v, g, cosine, sine, 1.0), raw_key, g_key)
    query_low = query_rot.astype(LOW)
    key_value = jnp.concatenate([key_rot.astype(LOW), value], axis=0)
    key_value = jnp.concatenate([key_value, to_partner(key_value)], axis=1)
    key_all, value_all = key_value[:head], key_value[head:]

    within = jnp.arange(share, dtype=jnp.int32)
    position = lambda c: jnp.concatenate([(r * COL + c) * share + within for r in chunk_rows])
    query_position = position(col)
    key_position = jnp.concatenate([query_position, position(1 - col)])
    offset = query_position[None, :] - key_position[:, None]
    allowed = (offset >= 0) & (offset < WINDOW)
    scores = jnp.where(allowed, dot(key_all, query_low, ((0,), (0,))), MASKED)
    weights = jnp.exp(scores - jnp.max(scores, axis=0, keepdims=True))
    probs = weights / jnp.sum(weights, axis=0, keepdims=True)
    probs_low = probs.astype(LOW)
    mixed = dot(value_all, probs_low, ((1,), (0,))).astype(LOW)
    branch = row_scatter(dot(out_weight, mixed, ((1,), (0,))))
    post_attn, post_factor = norm(branch, gain_post_attn)
    middle = x + post_attn
    ffn_norm, ffn_factor = norm(middle, gain_pre_ffn)
    ffn_in = row_gather(ffn_norm.astype(LOW))

    ffn_weight = assemble(ffn_own, ffn_mine, core)
    gate_weight, up_weight, down_t = [ffn_weight[:, i * wide : (i + 1) * wide] for i in range(3)]
    gate = dot(gate_weight, ffn_in, ((0,), (0,)))
    up = dot(up_weight, ffn_in, ((0,), (0,)))
    hidden, geglu_pull = jax.vjp(geglu, gate, up)
    hidden = hidden.astype(LOW)
    down_proj = row_scatter(dot(down_t, hidden, ((1,), (0,))))
    post_ffn, post_ffn_factor = norm(down_proj, gain_post_ffn)
    block_out = back_together((middle + post_ffn).astype(LOW))

    upstream = jnp.concatenate(spread(cotangent[0].T), axis=0).astype(WIDE)
    grad_down, grad_g_post_ffn = norm_back(down_proj, post_ffn_factor, gain_post_ffn, upstream)
    grad_down = row_gather(grad_down.astype(LOW))
    grad_gate, grad_up = geglu_pull(dot(down_t, grad_down, ((0,), (0,))))
    grad_gate, grad_up = grad_gate.astype(LOW), grad_up.astype(LOW)
    grad_ffn_in = row_scatter(
        dot(gate_weight, grad_gate, ((1,), (0,))) + dot(up_weight, grad_up, ((1,), (0,)))
    )
    grad_w_down = reduce_weight(dot(grad_down, hidden, ((1,), (1,))).astype(LOW), place)
    grad_w_gate = reduce_weight(dot(ffn_in, grad_gate, ((1,), (1,))).astype(LOW), place)
    grad_w_up = reduce_weight(dot(ffn_in, grad_up, ((1,), (1,))).astype(LOW), place)

    grad_mid_norm, grad_g_pre_ffn = norm_back(middle, ffn_factor, gain_pre_ffn, grad_ffn_in)
    grad_middle = upstream + grad_mid_norm
    grad_branch, grad_g_post_attn = norm_back(branch, post_factor, gain_post_attn, grad_middle)
    grad_branch = row_gather(grad_branch.astype(LOW))
    grad_w_out = dot(grad_branch, mixed, ((1,), (1,))).astype(LOW)
    grad_mixed = dot(out_weight, grad_branch, ((0,), (0,))).astype(LOW)

    grad_probs = dot(value_all, grad_mixed, ((0,), (0,)))
    grad_value_all = dot(grad_mixed, probs_low, ((1,), (1,)))
    grad_scores = (
        probs * (grad_probs - jnp.sum(probs * grad_probs, axis=0, keepdims=True))
    ).astype(LOW)
    grad_query_rot = dot(key_all, grad_scores, ((1,), (0,)))
    grad_key_all = dot(query_low, grad_scores, ((1,), (1,)))
    grad_kv_all = jnp.concatenate([grad_key_all, grad_value_all], axis=0)
    count = grad_kv_all.shape[1] // 2
    grad_kv = grad_kv_all[:, :count] + to_partner(grad_kv_all[:, count:].astype(LOW)).astype(WIDE)
    grad_query, grad_g_query = query_pull(grad_query_rot)
    grad_key, grad_g_key = key_pull(grad_kv[:head])
    grad_query = grad_query.astype(LOW)
    grad_kv = jnp.concatenate([grad_key, grad_kv[head:]], axis=0).astype(LOW)
    grad_qkv = jnp.concatenate([grad_query, grad_kv], axis=0)

    grad_attn_part = dot(qkv_weight, grad_qkv, ((1,), (0,)))
    grad_attn_in = row_scatter(grad_attn_part)
    grad_in_norm, _ = norm_back(x, attn_factor, gain_in, grad_attn_in)
    grad_inputs = back_together((grad_middle + grad_in_norm).astype(LOW))
    grad_g_in = jnp.sum(grad_attn_part * attn_in.astype(WIDE), axis=1) / gain_in[:, 0]

    quarters = grad_kv.reshape(ROW, -1, count)
    quarter = pick(quarters, row, 0).astype(WIDE)
    order = (0, -1, 1, 2)
    for distance in (1, 2, 3):
        given = row_shift(pick(quarters, (row + distance) % ROW, 0), distance)
        theirs = [(step - distance) % ROW for step in order]
        chunks = [given[:, i * share : (i + 1) * share] for i in range(ROW)]
        chunks = [chunks[theirs.index(step % ROW)] for step in order]
        quarter = quarter + jnp.concatenate(chunks, axis=1).astype(WIDE)
    grad_last = jnp.concatenate(
        [
            grad_w_out,
            dot(attn_in, jnp.concatenate([grad_query, quarter.astype(LOW)], axis=0), ((1,), (1,))).astype(LOW),
        ],
        axis=1,
    )
    slack = -grad_last.shape[1] % 256
    grad_last = reduce_weight(jnp.pad(grad_last, ((0, 0), (0, slack))), place)
    grad_w_out = grad_last[:, :head]
    grad_w_query = grad_last[:, head : 2 * head]
    quarter = grad_last[:, 2 * head : 2 * head + 2 * head // ROW]
    by_row = jnp.stack(
        [quarter, row_shift(quarter, 1), row_shift(quarter, 2), row_shift(quarter, 3)]
    )
    grad_w_kv = jnp.concatenate([pick(by_row, (row - r) % ROW, 0) for r in range(ROW)], axis=1)

    feature_gains = jnp.stack([grad_g_in, grad_g_post_attn, grad_g_pre_ffn, grad_g_post_ffn])
    head_gains = jnp.stack([grad_g_query, grad_g_key])
    head_gains = jnp.pad(head_gains, ((0, 0), (0, features - head)))
    summed = reduce_gains(
        jnp.concatenate(
            [feature_gains.reshape(4, COL, features).swapaxes(0, 1), head_gains[:, None]], axis=1
        )
    )

    whole = lambda w: w[:, :hidden_share].astype(WIDE)
    return (
        block_out.T[None],
        grad_inputs.T[None],
        grad_w_query.astype(WIDE),
        grad_w_kv[:, :head].astype(WIDE),
        grad_w_kv[:, head:].astype(WIDE),
        grad_w_out.astype(WIDE).T,
        whole(grad_w_gate),
        whole(grad_w_up),
        whole(grad_w_down).T,
        summed[0, 0],
        summed[0, 4, :head],
        summed[1, 4, :head],
        summed[0, 1],
        summed[0, 2],
        summed[0, 3],
    )


def solution(mesh):
    placed = (
        P("dp", "row", "col"),
        P("col", "row"),
        P("col", None),
        P("col", None),
        P("row", "col"),
        P("col", "row"),
        P("col", "row"),
        P("row", "col"),
        P("col"),
        P(),
        P(),
        P("col"),
        P("col"),
        P("col"),
        P("dp", "row", "col"),
    )
    return jax.shard_map(
        local,
        mesh=mesh,
        in_specs=placed,
        out_specs=(
            P("dp", "row", "col"),
            P("dp", "row", "col"),
            P("col", "row"),
            P("col", None),
            P("col", None),
            P("row", "col"),
            P("col", "row"),
            P("col", "row"),
            P("row", "col"),
            P("col"),
            P(),
            P(),
            P("col"),
            P("col"),
            P("col"),
        ),
        check_vma=False,
    )
```

```python
import jax
import jax.numpy as jnp
import numpy as np
from jax import lax
from jax.experimental import pallas as pl
from jax.experimental.pallas import tpu as pltpu
from jax.sharding import PartitionSpec as P

WINDOW = 512
EPSILON = 1e-06
MASKED = -1e30
ROPE_BASE = 10000.0
LOW = jnp.bfloat16
WIDE = jnp.float32

Y, HI, CORE, COL, ROW = 4, 2, 2, 2, 4


def device(y, z, core):
    return ((y * HI + z // COL) * CORE + core) * COL + z % COL


def z_route(shift_of):
    return [
        (device(y, z, core), device(y, (z + shift_of(z, core)) % 4, core))
        for y in range(Y)
        for z in range(4)
        for core in range(CORE)
    ]


def dp_route(target):
    return [(i, target(i)) for i in range(Y * HI * CORE)]


def by_z(shift_of):
    route = z_route(shift_of)
    return lambda v: lax.ppermute(v, ("dp", "col"), route)


to_partner = by_z(lambda z, core: 1 if z % 2 == 0 else -1)
to_cross = by_z(lambda z, core: -1 if z % 2 == 0 else 1)
to_opposite = by_z(lambda z, core: 2)
z_ring = by_z(lambda z, core: -1 if core == 0 else 1)


def core_swap(v):
    return lax.ppermute(v, "dp", dp_route(lambda i: i ^ 1))


def y_ring(v):
    step = HI * CORE
    return lax.ppermute(
        v, "dp", dp_route(lambda i: (i + (step if i % 2 == 0 else -step)) % (Y * step))
    )


def y_shift(v, distance):
    step = HI * CORE * distance
    return lax.ppermute(v, "dp", dp_route(lambda i: (i + step) % (Y * HI * CORE)))


def row_shift(v, distance):
    return lax.ppermute(v, "row", [(i, (i + distance) % ROW) for i in range(ROW)])


def row_gather(v):
    return jnp.concatenate([v, row_shift(v, 1), row_shift(v, -1), row_shift(v, 2)], axis=1)


def row_scatter(total):
    share = total.shape[1] // ROW
    own, *others = [total[:, i * share : (i + 1) * share] for i in range(ROW)]
    for part, distance in ((others[2], 2), (others[0], -1), (others[1], 1)):
        own = own + row_shift(part.astype(LOW), distance).astype(WIDE)
    return own


def dot(left, right, dims):
    return lax.dot_general(left, right, (dims, ((), ())), preferred_element_type=WIDE)


def norm(v, gain):
    factor = lax.rsqrt(jnp.sum(v * v, axis=0, keepdims=True) / v.shape[0] + EPSILON)
    return v * factor * gain, factor


def norm_back(v, factor, gain, upstream):
    scaled = upstream * gain
    inner = jnp.sum(scaled * v, axis=0, keepdims=True)
    grad = factor * scaled - v * (factor * factor * factor) * inner / v.shape[0]
    return grad, jnp.sum(upstream * v * factor, axis=1)


def head_map(raw, gain, cosine, sine, scaling):
    normed = (
        raw * lax.rsqrt(jnp.mean(raw * raw, axis=0, keepdims=True) + EPSILON) * gain[:, None]
    )
    half = raw.shape[0] // 2
    first, second = normed[:half], normed[half:]
    turned = jnp.concatenate(
        [first * cosine - second * sine, second * cosine + first * sine], axis=0
    )
    return turned * scaling


def geglu(gate, up):
    return jax.nn.gelu(gate, approximate=True) * up


def rope_tables(length, head_size):
    half = head_size // 2
    exponent = np.arange(half, dtype=np.float32) * np.float32(2.0 / head_size)
    rate = np.float32(ROPE_BASE) ** (-exponent)
    angles = rate[:, None] * np.arange(length, dtype=np.float32)[None, :]
    return np.stack([np.cos(angles), np.sin(angles)]).astype(np.float32)


def pick(v, index, axis):
    return lax.dynamic_index_in_dim(v, index, axis, keepdims=False)


def pack_kernel(core, *refs):
    *parts, packed = refs
    for i, part in enumerate(parts):

        @pl.when(pl.program_id(0) == i)
        def _():
            packed[...] = part[...]


def pack(core, weights):
    rows, width = weights[0].shape[0] // 2, weights[0].shape[1]
    count = len(weights)
    block = (rows, width)
    return pl.pallas_call(
        pack_kernel,
        grid_spec=pltpu.PrefetchScalarGridSpec(
            num_scalar_prefetch=1,
            grid=(count,),
            in_specs=[pl.BlockSpec(block, lambda i, core: (core[0], 0))] * count,
            out_specs=pl.BlockSpec(block, lambda i, core: (i, 0)),
        ),
        out_shape=jax.ShapeDtypeStruct((count * rows, width), weights[0].dtype),
        compiler_params=pltpu.CompilerParams(vmem_limit_bytes=32 * 2**20),
        cost_estimate=pl.CostEstimate(
            flops=0, bytes_accessed=4 * count * rows * width, transcendentals=0
        ),
    )(core.reshape(1), *weights)


def join_kernel(count, core, *refs):
    owns, mine, theirs, wholes = refs[:count], refs[count], refs[count + 1], refs[count + 2 :]
    step = pl.program_id(0)
    rows = owns[0].shape[0]
    for i in range(count):

        @pl.when(step % 2 == 0)
        def _():
            wholes[i][...] = owns[i][...]

        @pl.when(step == 1)
        def _():
            wholes[i][...] = mine[i * rows : (i + 1) * rows]

        @pl.when(step == 3)
        def _():
            wholes[i][...] = theirs[i * rows : (i + 1) * rows]


def join(core, owns, mine, theirs):
    count = len(owns)
    rows, width = owns[0].shape[0] // 2, owns[0].shape[1]
    block = (rows, width)
    parts = pl.BlockSpec((count * rows, width), lambda i, core: (0, 0))
    own = pl.BlockSpec(block, lambda i, core: (jnp.where(i < 2, core[0], 1 - core[0]), 0))
    return pl.pallas_call(
        lambda *refs: join_kernel(count, *refs),
        grid_spec=pltpu.PrefetchScalarGridSpec(
            num_scalar_prefetch=1,
            grid=(4,),
            in_specs=[own] * count + [parts, parts],
            out_specs=[pl.BlockSpec(block, lambda i, core: (i, 0))] * count,
        ),
        out_shape=[jax.ShapeDtypeStruct((4 * rows, width), owns[0].dtype)] * count,
        compiler_params=pltpu.CompilerParams(vmem_limit_bytes=40 * 2**20),
        cost_estimate=pl.CostEstimate(
            flops=0, bytes_accessed=16 * count * rows * width, transcendentals=0
        ),
    )(core.reshape(1), *owns, mine, theirs)


def add(a, b):
    return (a.astype(WIDE) + b.astype(WIDE)).astype(LOW)


Y_GROUPS = [[y * HI * CORE + i for y in range(Y)] for i in range(HI * CORE)]


class Sum:
    def __init__(self, left, right, place):
        self.y, self.z, self.core = place
        rows, self.width = left.shape[0] // 2, right.shape[0]
        product = lambda part: dot(part, right, ((1,), (1,))).astype(LOW)
        self.given, self.kept = product(left[rows:]), product(left[:rows])

    def over_cores(self):
        held = add(self.kept, core_swap(self.given))
        self.held = held.reshape(COL, Y, -1, self.width).swapaxes(0, 1)

    def over_y(self):
        self.total = lax.psum_scatter(
            self.held.reshape(-1, self.width),
            "dp",
            scatter_dimension=0,
            axis_index_groups=Y_GROUPS,
            tiled=True,
        ).reshape(COL, -1, self.width)

    def over_y_directly(self):
        chunk = lambda distance: pick(self.held, (self.y + distance) % Y, 0)
        total = chunk(0).astype(WIDE)
        for distance in (2, 1, 3):
            total = total + y_shift(chunk(distance), distance).astype(WIDE)
        self.total = total.astype(LOW)

    def over_z(self):
        own, other = self.total[0], self.total[1]
        self.total = (
            own.astype(WIDE)
            + to_opposite(own).astype(WIDE)
            + to_partner(other).astype(WIDE)
            + to_cross(other).astype(WIDE)
        ).astype(LOW)

    def over_row(self, start):
        sent = self.total[:, start:]
        part = sent.astype(WIDE)
        for distance in (2, 1, 3):
            part = part + row_shift(sent, distance).astype(WIDE)
        self.total = jnp.concatenate([self.total[:, :start], part.astype(LOW)], axis=1)

    def share_y_nearest(self):
        self.near = y_shift(self.total, 1), y_shift(self.total, -1)

    def share_y_farthest(self):
        below, above = self.near
        half = self.width // 2
        across = jnp.concatenate(
            [y_shift(below[:, :half], 1), y_shift(above[:, half:], -1)], axis=1
        )
        self.lay_y(self.total, below, across, above)

    def share_y(self):
        self.lay_y(self.total, *[y_shift(self.total, distance) for distance in (1, 2, 3)])

    def lay_y(self, *parts):
        ring = jnp.stack(parts)
        self.mine = jnp.concatenate([pick(ring, (self.y - j) % Y, 0) for j in range(Y)], axis=0)

    def share_cores(self):
        theirs = core_swap(self.mine)
        first = jnp.where(self.core == 0, self.mine, theirs)
        second = jnp.where(self.core == 0, theirs, self.mine)
        return jnp.concatenate([first, second], axis=0)


class Small(Sum):
    def __init__(self, given, kept, place):
        self.y, self.z, self.core = place
        self.given, self.kept, self.width = given, kept, given.shape[1]


def local(
    inputs,
    w_query,
    w_key,
    w_value,
    attention_output_weight,
    w_gate,
    w_up,
    down_weight,
    g_in,
    g_query,
    g_key,
    g_post_attn,
    g_pre_ffn,
    g_post_ffn,
    cotangent,
):
    col, row, dp = lax.axis_index("col"), lax.axis_index("row"), lax.axis_index("dp")
    core, hi, y = dp % CORE, (dp // CORE) % HI, dp // (HI * CORE)
    place = (y, hi * COL + col, core)
    features, share = inputs.shape[2], inputs.shape[1] // COL
    head = g_query.shape[0]
    hidden_share = w_gate.shape[1]
    wide = hidden_share + -hidden_share % 256
    barrier = lax.optimization_barrier

    def mix(own, other):
        halves = jnp.stack([own, other]).reshape(COL, CORE, -1, own.shape[1]).swapaxes(0, 1)
        return jnp.where(core == 0, halves, halves[::-1]).reshape(-1, own.shape[1])

    def unmix(v):
        halves = v.reshape(CORE, COL, -1, v.shape[1])
        halves = jnp.where(core == 0, halves, halves[::-1]).swapaxes(0, 1)
        return halves.reshape(COL, -1, v.shape[1])

    def spread(v):
        kept = lax.dynamic_slice_in_dim(v, col * share, share, 1)
        given = lax.dynamic_slice_in_dim(v, (1 - col) * share, share, 1)
        return kept, to_partner(given)

    def back_together(v):
        kept, given = unmix(v)
        theirs = to_partner(given)
        return jnp.where(
            col == 0,
            jnp.concatenate([kept, theirs], axis=1),
            jnp.concatenate([theirs, kept], axis=1),
        )

    kept, taken = spread(inputs[0].T)
    gains_own = jnp.stack([g_in, g_post_attn, g_pre_ffn, g_post_ffn])
    gains_other = to_partner(gains_own)
    gains = mix(gains_own.T, gains_other.T)
    gain_in, gain_post_attn, gain_pre_ffn, gain_post_ffn = [gains[:, i : i + 1] for i in range(4)]

    attn_own = jnp.concatenate([w_query, w_key, w_value, attention_output_weight.T], axis=1)
    ffn_own = (w_gate, w_up, down_weight.T)
    attn_mine = z_ring(pack(core, [attn_own]))
    ffn_mine = z_ring(pack(core, ffn_own))
    (attn_weight,) = join(core, [attn_own], attn_mine, core_swap(attn_mine))
    qkv_weight, out_weight = attn_weight[:, : 3 * head], attn_weight[:, 3 * head :]

    x = mix(kept, taken).astype(WIDE)
    attn_norm, attn_factor = norm(x, gain_in)
    attn_in = row_gather(attn_norm.astype(LOW))
    qkv = dot(qkv_weight, attn_in, ((0,), (0,)))
    raw_query, raw_key, value = qkv[:head], qkv[head : 2 * head], qkv[2 * head :].astype(LOW)

    chunk_rows = [row, (row - 1) % ROW, (row + 1) % ROW, (row + 2) % ROW]
    tables = jnp.asarray(rope_tables(ROW * COL * share, head))
    turns = jnp.concatenate(
        [
            lax.dynamic_slice_in_dim(tables, (r * COL + col) * share, share, 2)
            for r in chunk_rows
        ],
        axis=2,
    )
    cosine, sine = turns[0], turns[1]
    query_rot, query_pull = jax.vjp(
        lambda v, g: head_map(v, g, cosine, sine, head**-0.5), raw_query, g_query
    )
    key_rot, key_pull = jax.vjp(lambda v, g: head_map(v, g, cosine, sine, 1.0), raw_key, g_key)
    query_low = query_rot.astype(LOW)
    key_value = jnp.concatenate([key_rot.astype(LOW), value], axis=0)
    key_value_other, ffn_mine = barrier((to_partner(key_value), ffn_mine))
    key_value = jnp.concatenate([key_value, key_value_other], axis=1)
    key_all, value_all = key_value[:head], key_value[head:]

    within = jnp.arange(share, dtype=jnp.int32)
    position = lambda c: jnp.concatenate([(r * COL + c) * share + within for r in chunk_rows])
    query_position = position(col)
    key_position = jnp.concatenate([query_position, position(1 - col)])
    offset = query_position[None, :] - key_position[:, None]
    allowed = (offset >= 0) & (offset < WINDOW)
    scores = jnp.where(allowed, dot(key_all, query_low, ((0,), (0,))), MASKED)
    weights = jnp.exp(scores - jnp.max(scores, axis=0, keepdims=True))
    probs = weights / jnp.sum(weights, axis=0, keepdims=True)
    probs_low = probs.astype(LOW)
    mixed = dot(value_all, probs_low, ((1,), (0,))).astype(LOW)
    branch_part = dot(out_weight, mixed, ((1,), (0,)))
    branch = row_scatter(branch_part)
    gate_weight, up_weight, down_t = join(core, ffn_own, ffn_mine, core_swap(ffn_mine))
    post_attn, post_factor = norm(branch, gain_post_attn)
    middle = x + post_attn
    ffn_norm, ffn_factor = norm(middle, gain_pre_ffn)
    ffn_in = row_gather(ffn_norm.astype(LOW))

    gate = dot(gate_weight, ffn_in, ((0,), (0,)))
    up = dot(up_weight, ffn_in, ((0,), (0,)))
    hidden, geglu_pull = jax.vjp(geglu, gate, up)
    hidden = hidden.astype(LOW)
    down_proj = row_scatter(dot(down_t, hidden, ((1,), (0,))))
    post_ffn, post_ffn_factor = norm(down_proj, gain_post_ffn)
    block_out = back_together((middle + post_ffn).astype(LOW))

    kept, taken = spread(cotangent[0].T)
    upstream = mix(kept, taken).astype(WIDE)
    grad_down, grad_g_post_ffn = norm_back(down_proj, post_ffn_factor, gain_post_ffn, upstream)
    grad_down = row_gather(grad_down.astype(LOW))
    more = lambda v: jnp.pad(v, ((0, wide - hidden_share), (0, 0)))
    sum_down = Sum(grad_down, more(hidden), place)
    sum_down.given, grad_down = barrier((sum_down.given, grad_down))
    sum_down.over_cores()
    sum_down.over_y()
    grad_gate, grad_up = geglu_pull(dot(down_t, grad_down, ((0,), (0,))))
    grad_gate, grad_up = grad_gate.astype(LOW), grad_up.astype(LOW)
    grad_pair = jnp.concatenate([more(grad_gate), more(grad_up)], axis=0)
    sum_pair = Sum(ffn_in, grad_pair, place)
    sum_pair.given, grad_gate, grad_up = barrier((sum_pair.given, grad_gate, grad_up))
    sum_pair.over_cores()
    grad_ffn_in = row_scatter(
        dot(gate_weight, grad_gate, ((1,), (0,))) + dot(up_weight, grad_up, ((1,), (0,)))
    )

    grad_mid_norm, grad_g_pre_ffn = norm_back(middle, ffn_factor, gain_pre_ffn, grad_ffn_in)
    grad_middle = upstream + grad_mid_norm
    grad_branch, grad_g_post_attn = norm_back(branch, post_factor, gain_post_attn, grad_middle)
    grad_branch, sum_pair.held, sum_down.total = barrier(
        (grad_branch.astype(LOW), sum_pair.held, sum_down.total)
    )
    sum_pair.over_y()
    grad_branch = row_gather(grad_branch)
    sum_down.over_z()
    grad_mixed = dot(out_weight, grad_branch, ((0,), (0,))).astype(LOW)

    grad_probs = dot(value_all, grad_mixed, ((0,), (0,)))
    grad_value_all = dot(grad_mixed, probs_low, ((1,), (1,)))
    grad_scores = (
        probs * (grad_probs - jnp.sum(probs * grad_probs, axis=0, keepdims=True))
    ).astype(LOW)
    grad_query_rot = dot(key_all, grad_scores, ((1,), (0,)))
    grad_key_all = dot(query_low, grad_scores, ((1,), (1,)))
    grad_kv_all = jnp.concatenate([grad_key_all, grad_value_all], axis=0)
    count = grad_kv_all.shape[1] // 2
    grad_kv = grad_kv_all[:, :count] + to_partner(grad_kv_all[:, count:].astype(LOW)).astype(WIDE)
    grad_query, grad_g_query = query_pull(grad_query_rot)
    grad_key, grad_g_key = key_pull(grad_kv[:head])
    grad_query = grad_query.astype(LOW)
    grad_kv = jnp.concatenate([grad_key, grad_kv[head:]], axis=0).astype(LOW)
    grad_qkv = jnp.concatenate([grad_query, grad_kv], axis=0)
    grad_qkv, sum_down.total = barrier((grad_qkv, sum_down.total))
    sum_down.share_y_nearest()

    grad_attn_part = dot(qkv_weight, grad_qkv, ((1,), (0,)))
    grad_attn_in = row_scatter(grad_attn_part)
    grad_g_in = jnp.sum(grad_attn_part * attn_in.astype(WIDE), axis=1) / gain_in[:, 0]

    head_gains = jnp.pad(
        jnp.stack([grad_g_query, grad_g_key], axis=1), ((0, features - head), (0, 0))
    )
    head_gains = mix(head_gains, head_gains)
    grad_gains = jnp.concatenate(
        [
            jnp.stack([grad_g_in, grad_g_post_attn, grad_g_pre_ffn, grad_g_post_ffn], axis=1),
            head_gains,
        ],
        axis=1,
    )
    slack = -grad_gains.shape[1] % 128
    gain_columns = jnp.pad(grad_gains, ((0, 0), (0, slack))).astype(LOW)

    def small_part(rows):
        return jnp.concatenate(
            [
                dot(attn_in[rows], grad_query, ((1,), (1,))).astype(LOW),
                dot(grad_branch[rows], mixed, ((1,), (1,))).astype(LOW),
                dot(attn_in[rows], grad_kv, ((1,), (1,))).astype(LOW),
                gain_columns[rows],
            ],
            axis=1,
        )

    sum_small = Small(small_part(slice(features, None)), small_part(slice(features)), place)
    sum_small.over_cores()
    grad_attn_in, sum_small.held, sum_pair.total, sum_down.near = barrier(
        (grad_attn_in, sum_small.held, sum_pair.total, sum_down.near)
    )
    sum_small.over_y_directly()
    sum_pair.over_z()
    sum_down.share_y_farthest()
    grad_in_norm, _ = norm_back(x, attn_factor, gain_in, grad_attn_in)
    grad_inputs = back_together((grad_middle + grad_in_norm).astype(LOW))
    sum_pair.share_y_nearest()
    sum_small.total, sum_pair.near = barrier((sum_small.total, sum_pair.near))
    sum_pair.share_y_farthest()
    sum_small.over_z()
    sum_small.over_row(2 * head)
    sum_small.share_y()
    small = sum_small.share_cores()
    grad_w_down = sum_down.share_cores()
    grad_w_pair = sum_pair.share_cores()
    grad_w_gate, grad_w_up = grad_w_pair[:, :wide], grad_w_pair[:, wide:]
    grad_w_query, grad_w_out = small[:, :head], small[:, head : 2 * head]
    grad_w_key, grad_w_value = small[:, 2 * head : 3 * head], small[:, 3 * head : 4 * head]
    summed = small[:, 4 * head : 4 * head + 6].astype(WIDE).T

    whole = lambda w: w[:, :hidden_share].astype(WIDE)
    return (
        block_out.T[None],
        grad_inputs.T[None],
        grad_w_query.astype(WIDE),
        grad_w_key.astype(WIDE),
        grad_w_value.astype(WIDE),
        grad_w_out.astype(WIDE).T,
        whole(grad_w_gate),
        whole(grad_w_up),
        whole(grad_w_down).T,
        summed[0],
        summed[4, :head],
        summed[5, :head],
        summed[1],
        summed[2],
        summed[3],
    )


def solution(mesh):
    placed = (
        P("dp", "row", "col"),
        P("col", "row"),
        P("col", None),
        P("col", None),
        P("row", "col"),
        P("col", "row"),
        P("col", "row"),
        P("row", "col"),
        P("col"),
        P(),
        P(),
        P("col"),
        P("col"),
        P("col"),
        P("dp", "row", "col"),
    )
    return jax.shard_map(
        local,
        mesh=mesh,
        in_specs=placed,
        out_specs=(
            P("dp", "row", "col"),
            P("dp", "row", "col"),
            P("col", "row"),
            P("col", None),
            P("col", None),
            P("row", "col"),
            P("col", "row"),
            P("col", "row"),
            P("row", "col"),
            P("col"),
            P(),
            P(),
            P("col"),
            P("col"),
            P("col"),
        ),
        check_vma=False,
    )
```

```python
import jax
import jax.numpy as jnp
import numpy as np
from jax import lax
from jax.experimental import pallas as pl
from jax.experimental.pallas import tpu as pltpu
from jax.sharding import PartitionSpec as P

WINDOW = 512
EPSILON = 1e-06
MASKED = -1e30
ROPE_BASE = 10000.0
LOW = jnp.bfloat16
WIDE = jnp.float32

Y, HI, CORE, COL, ROW = 4, 2, 2, 2, 4


def device(y, z, core):
    return ((y * HI + z // COL) * CORE + core) * COL + z % COL


def z_route(shift_of):
    return [
        (device(y, z, core), device(y, (z + shift_of(z, core)) % 4, core))
        for y in range(Y)
        for z in range(4)
        for core in range(CORE)
    ]


def dp_route(target):
    return [(i, target(i)) for i in range(Y * HI * CORE)]


def by_z(shift_of):
    route = z_route(shift_of)
    return lambda v: lax.ppermute(v, ("dp", "col"), route)


to_partner = by_z(lambda z, core: 1 if z % 2 == 0 else -1)
to_cross = by_z(lambda z, core: -1 if z % 2 == 0 else 1)
to_opposite = by_z(lambda z, core: 2)
z_ring = by_z(lambda z, core: -1 if core == 0 else 1)


def core_swap(v):
    return lax.ppermute(v, "dp", dp_route(lambda i: i ^ 1))


def y_ring(v):
    step = HI * CORE
    return lax.ppermute(
        v, "dp", dp_route(lambda i: (i + (step if i % 2 == 0 else -step)) % (Y * step))
    )


def y_shift(v, distance):
    step = HI * CORE * distance
    return lax.ppermute(v, "dp", dp_route(lambda i: (i + step) % (Y * HI * CORE)))


def row_shift(v, distance):
    return lax.ppermute(v, "row", [(i, (i + distance) % ROW) for i in range(ROW)])


def row_gather(v):
    return jnp.concatenate([v, row_shift(v, 1), row_shift(v, -1), row_shift(v, 2)], axis=1)


def row_scatter_parts(total):
    share = total.shape[1] // ROW
    own, *others = [total[:, i * share : (i + 1) * share] for i in range(ROW)]
    return [own] + [
        row_shift(part.astype(LOW), distance)
        for part, distance in ((others[2], 2), (others[0], -1), (others[1], 1))
    ]


def row_scatter(total):
    own, *parts = row_scatter_parts(total)
    for part in parts:
        own = own + part.astype(WIDE)
    return own


def dot(left, right, dims):
    return lax.dot_general(left, right, (dims, ((), ())), preferred_element_type=WIDE)


def norm(v, gain):
    factor = lax.rsqrt(jnp.sum(v * v, axis=0, keepdims=True) / v.shape[0] + EPSILON)
    return v * factor * gain, factor


def norm_back(v, factor, gain, upstream):
    scaled = upstream * gain
    inner = jnp.sum(scaled * v, axis=0, keepdims=True)
    grad = factor * scaled - v * (factor * factor * factor) * inner / v.shape[0]
    return grad, jnp.sum(upstream * v * factor, axis=1)


def head_map(raw, gain, cosine, sine, scaling):
    normed = (
        raw * lax.rsqrt(jnp.mean(raw * raw, axis=0, keepdims=True) + EPSILON) * gain[:, None]
    )
    half = raw.shape[0] // 2
    first, second = normed[:half], normed[half:]
    turned = jnp.concatenate(
        [first * cosine - second * sine, second * cosine + first * sine], axis=0
    )
    return turned * scaling


def geglu(gate, up):
    return jax.nn.gelu(gate, approximate=True) * up


def rope_tables(length, head_size):
    half = head_size // 2
    exponent = np.arange(half, dtype=np.float32) * np.float32(2.0 / head_size)
    rate = np.float32(ROPE_BASE) ** (-exponent)
    angles = rate[:, None] * np.arange(length, dtype=np.float32)[None, :]
    return np.stack([np.cos(angles), np.sin(angles)]).astype(np.float32)


def pick(v, index, axis):
    return lax.dynamic_index_in_dim(v, index, axis, keepdims=False)


def pack_kernel(core, weight, packed):
    packed[...] = weight[...]


def pack(core, weight):
    block = (weight.shape[0] // 2, weight.shape[1])
    return pl.pallas_call(
        pack_kernel,
        grid_spec=pltpu.PrefetchScalarGridSpec(
            num_scalar_prefetch=1,
            grid=(1,),
            in_specs=[pl.BlockSpec(block, lambda i, core: (core[0], 0))],
            out_specs=pl.BlockSpec(block, lambda i, core: (0, 0)),
        ),
        out_shape=jax.ShapeDtypeStruct(block, weight.dtype),
        compiler_params=pltpu.CompilerParams(vmem_limit_bytes=16 * 2**20),
        cost_estimate=pl.CostEstimate(
            flops=0, bytes_accessed=4 * block[0] * block[1], transcendentals=0
        ),
    )(core.reshape(1), weight)


def join_kernel(count, core, *refs):
    owns, mine, theirs, wholes = [refs[i * count : (i + 1) * count] for i in range(4)]
    step = pl.program_id(0)
    for i in range(count):

        @pl.when(step % 2 == 0)
        def _():
            wholes[i][...] = owns[i][...]

        @pl.when(step == 1)
        def _():
            wholes[i][...] = mine[i][...]

        @pl.when(step == 3)
        def _():
            wholes[i][...] = theirs[i][...]


def join(core, owns, mine, theirs):
    count = len(owns)
    block = (owns[0].shape[0] // 2, owns[0].shape[1])
    part = pl.BlockSpec(block, lambda i, core: (0, 0))
    own = pl.BlockSpec(block, lambda i, core: (jnp.where(i < 2, core[0], 1 - core[0]), 0))
    return pl.pallas_call(
        lambda *refs: join_kernel(count, *refs),
        grid_spec=pltpu.PrefetchScalarGridSpec(
            num_scalar_prefetch=1,
            grid=(4,),
            in_specs=[own] * count + [part] * (2 * count),
            out_specs=[pl.BlockSpec(block, lambda i, core: (i, 0))] * count,
        ),
        out_shape=[jax.ShapeDtypeStruct((4 * block[0], block[1]), owns[0].dtype)] * count,
        compiler_params=pltpu.CompilerParams(vmem_limit_bytes=40 * 2**20),
        cost_estimate=pl.CostEstimate(
            flops=0, bytes_accessed=16 * count * block[0] * block[1], transcendentals=0
        ),
    )(core.reshape(1), *owns, *mine, *theirs)


def add(a, b):
    return (a.astype(WIDE) + b.astype(WIDE)).astype(LOW)


Y_GROUPS = [[y * HI * CORE + i for y in range(Y)] for i in range(HI * CORE)]


class Sum:
    def __init__(self, left, right, place):
        self.y, self.z, self.core = place
        rows, self.width = left.shape[0] // 2, right.shape[0]
        product = lambda part: dot(part, right, ((1,), (1,))).astype(LOW)
        self.given, self.kept = product(left[rows:]), product(left[:rows])

    def over_cores(self):
        held = add(self.kept, core_swap(self.given))
        self.held = held.reshape(COL, Y, -1, self.width).swapaxes(0, 1)

    def over_y(self):
        self.total = lax.psum_scatter(
            self.held.reshape(-1, self.width),
            "dp",
            scatter_dimension=0,
            axis_index_groups=Y_GROUPS,
            tiled=True,
        ).reshape(COL, -1, self.width)

    def over_y_directly(self):
        chunk = lambda distance: pick(self.held, (self.y + distance) % Y, 0)
        total = chunk(0).astype(WIDE)
        for distance in (2, 1, 3):
            total = total + y_shift(chunk(distance), distance).astype(WIDE)
        self.total = total.astype(LOW)

    def over_z(self):
        total = add(self.total[0], to_partner(self.total[1]))
        self.total = add(total, to_opposite(total))

    def over_row(self, start):
        sent = self.total[:, start:]
        part = sent.astype(WIDE)
        for distance in (2, 1, 3):
            part = part + row_shift(sent, distance).astype(WIDE)
        self.total = jnp.concatenate([self.total[:, :start], part.astype(LOW)], axis=1)

    def share_y_nearest(self):
        self.near = y_shift(self.total, 1), y_shift(self.total, -1)

    def share_y_farthest(self):
        below, above = self.near
        half = self.width // 2
        across = jnp.concatenate(
            [y_shift(below[:, :half], 1), y_shift(above[:, half:], -1)], axis=1
        )
        self.lay_y(self.total, below, across, above)

    def share_y(self):
        self.lay_y(self.total, *[y_shift(self.total, distance) for distance in (1, 2, 3)])

    def lay_y(self, *parts):
        ring = jnp.stack(parts)
        self.mine = jnp.concatenate([pick(ring, (self.y - j) % Y, 0) for j in range(Y)], axis=0)

    def share_cores(self):
        theirs = core_swap(self.mine)
        first = jnp.where(self.core == 0, self.mine, theirs)
        second = jnp.where(self.core == 0, theirs, self.mine)
        return jnp.concatenate([first, second], axis=0)


class Small(Sum):
    def __init__(self, given, kept, place):
        self.y, self.z, self.core = place
        self.given, self.kept, self.width = given, kept, given.shape[1]


def local(
    inputs,
    w_query,
    w_key,
    w_value,
    attention_output_weight,
    w_gate,
    w_up,
    down_weight,
    g_in,
    g_query,
    g_key,
    g_post_attn,
    g_pre_ffn,
    g_post_ffn,
    cotangent,
):
    col, row, dp = lax.axis_index("col"), lax.axis_index("row"), lax.axis_index("dp")
    core, hi, y = dp % CORE, (dp // CORE) % HI, dp // (HI * CORE)
    place = (y, hi * COL + col, core)
    features, share = inputs.shape[2], inputs.shape[1] // COL
    head = g_query.shape[0]
    hidden_share = w_gate.shape[1]
    wide = hidden_share + -hidden_share % 256
    barrier = lax.optimization_barrier

    def mix(own, other):
        half = own.shape[0] // 2
        parts = [v[:half] for v in (own, other)], [v[half:] for v in (own, other)]
        first = [jnp.where(core == 0, a, b) for a, b in zip(*parts)]
        second = [jnp.where(core == 0, b, a) for a, b in zip(*parts)]
        return jnp.concatenate(first + second, axis=0)

    def unmix(v):
        half = v.shape[0] // 4
        own_a, other_a, own_b, other_b = [v[i * half : (i + 1) * half] for i in range(4)]
        lay = lambda a, b: jnp.concatenate(
            [jnp.where(core == 0, a, b), jnp.where(core == 0, b, a)], axis=0
        )
        return lay(own_a, own_b), lay(other_a, other_b)

    def spread(v):
        kept = lax.dynamic_slice_in_dim(v, col * share, share, 1)
        given = lax.dynamic_slice_in_dim(v, (1 - col) * share, share, 1)
        return kept, to_partner(given)

    def back_together(v):
        kept, given = unmix(v)
        theirs = to_partner(given)
        return jnp.where(
            col == 0,
            jnp.concatenate([kept, theirs], axis=1),
            jnp.concatenate([theirs, kept], axis=1),
        )

    kept, taken = spread(inputs[0].T)
    gains_own = jnp.stack([g_in, g_post_attn, g_pre_ffn, g_post_ffn])
    gains_other = to_partner(gains_own)
    gains = mix(gains_own.T, gains_other.T)
    gain_in, gain_post_attn, gain_pre_ffn, gain_post_ffn = [gains[:, i : i + 1] for i in range(4)]

    x = mix(kept, taken).astype(WIDE)
    attn_norm, attn_factor = norm(x, gain_in)
    attn_norm, w_query, w_gate = barrier((attn_norm.astype(LOW), w_query, w_gate))
    attn_in = row_gather(attn_norm)

    attn_own = jnp.concatenate([w_query, w_key, w_value, attention_output_weight.T], axis=1)
    attn_mine = z_ring(pack(core, attn_own))
    gate_mine = z_ring(pack(core, w_gate))
    up_sent, gate_mine = barrier((pack(core, w_up), gate_mine))
    up_mine = z_ring(up_sent)
    (attn_weight,) = join(core, [attn_own], [attn_mine], [core_swap(attn_mine)])
    qkv_weight, out_weight = attn_weight[:, : 3 * head], attn_weight[:, 3 * head :]

    qkv = dot(qkv_weight, attn_in, ((0,), (0,)))
    raw_query, raw_key, value = qkv[:head], qkv[head : 2 * head], qkv[2 * head :].astype(LOW)

    chunk_rows = [row, (row - 1) % ROW, (row + 1) % ROW, (row + 2) % ROW]
    tables = jnp.asarray(rope_tables(ROW * COL * share, head))
    turns = jnp.concatenate(
        [
            lax.dynamic_slice_in_dim(tables, (r * COL + col) * share, share, 2)
            for r in chunk_rows
        ],
        axis=2,
    )
    cosine, sine = turns[0], turns[1]
    query_rot, query_pull = jax.vjp(
        lambda v, g: head_map(v, g, cosine, sine, head**-0.5), raw_query, g_query
    )
    key_rot, key_pull = jax.vjp(lambda v, g: head_map(v, g, cosine, sine, 1.0), raw_key, g_key)
    query_low = query_rot.astype(LOW)
    key_value = jnp.concatenate([key_rot.astype(LOW), value], axis=0)
    key_value_other, down_sent = barrier((to_partner(key_value), pack(core, down_weight.T)))
    down_mine = z_ring(down_sent)
    key_value = jnp.concatenate([key_value, key_value_other], axis=1)
    key_all, value_all = key_value[:head], key_value[head:]

    steps = np.repeat(np.array([0, -1, 1, 2], np.int32), share)
    within = np.tile(np.arange(share, dtype=np.int32), ROW)
    position = lambda c: (((row + steps) % ROW) * COL + c) * share + within
    query_position = position(col)
    key_position = jnp.concatenate([query_position, position(1 - col)])
    offset = query_position[None, :] - key_position[:, None]
    allowed = (offset >= 0) & (offset < WINDOW)
    scores = jnp.where(allowed, dot(key_all, query_low, ((0,), (0,))), MASKED)
    weights = jnp.exp(scores - jnp.max(scores, axis=0, keepdims=True))
    probs = weights / jnp.sum(weights, axis=0, keepdims=True)
    probs_low = probs.astype(LOW)
    mixed = dot(value_all, probs_low, ((1,), (0,))).astype(LOW)
    branch_part = dot(out_weight, mixed, ((1,), (0,)))
    branch = row_scatter(branch_part)
    pair_mine = [gate_mine, up_mine]
    gate_weight, up_weight = join(
        core, [w_gate, w_up], pair_mine, [core_swap(part) for part in pair_mine]
    )
    down_mine, branch = barrier((down_mine, branch))
    (down_t,) = join(core, [down_weight.T], [down_mine], [core_swap(down_mine)])
    post_attn, post_factor = norm(branch, gain_post_attn)
    middle = x + post_attn
    ffn_norm, ffn_factor = norm(middle, gain_pre_ffn)
    ffn_in = row_gather(ffn_norm.astype(LOW))

    gate = dot(gate_weight, ffn_in, ((0,), (0,)))
    up = dot(up_weight, ffn_in, ((0,), (0,)))
    hidden, geglu_pull = jax.vjp(geglu, gate, up)
    hidden = hidden.astype(LOW)
    down_proj = row_scatter(dot(down_t, hidden, ((1,), (0,))))
    post_ffn, post_ffn_factor = norm(down_proj, gain_post_ffn)
    block_out = back_together((middle + post_ffn).astype(LOW))

    kept, taken = spread(cotangent[0].T)
    upstream = mix(kept, taken).astype(WIDE)
    grad_down, grad_g_post_ffn = norm_back(down_proj, post_ffn_factor, gain_post_ffn, upstream)
    grad_down = row_gather(grad_down.astype(LOW))
    more = lambda v: jnp.pad(v, ((0, wide - hidden_share), (0, 0)))
    sum_down = Sum(grad_down, more(hidden), place)
    sum_down.given, grad_down = barrier((sum_down.given, grad_down))
    sum_down.over_cores()
    sum_down.over_y()
    grad_gate, grad_up = geglu_pull(dot(down_t, grad_down, ((0,), (0,))))
    grad_gate, grad_up = grad_gate.astype(LOW), grad_up.astype(LOW)
    grad_pair = jnp.concatenate([more(grad_gate), more(grad_up)], axis=0)
    grad_pair, grad_gate, grad_up = barrier((grad_pair, grad_gate, grad_up))
    sum_pair = Sum(ffn_in, grad_pair, place)
    sum_pair.given, grad_gate, grad_up = barrier((sum_pair.given, grad_gate, grad_up))
    sum_pair.over_cores()
    own, far, left, right = row_scatter_parts(
        dot(gate_weight, grad_gate, ((1,), (0,))) + dot(up_weight, grad_up, ((1,), (0,)))
    )
    own, sum_pair.held = barrier((own, sum_pair.held))
    sum_pair.over_y()
    grad_ffn_in = own + left.astype(WIDE) + right.astype(WIDE) + far.astype(WIDE)

    grad_mid_norm, grad_g_pre_ffn = norm_back(middle, ffn_factor, gain_pre_ffn, grad_ffn_in)
    grad_middle = upstream + grad_mid_norm
    grad_branch, grad_g_post_attn = norm_back(branch, post_factor, gain_post_attn, grad_middle)
    grad_branch = row_gather(grad_branch.astype(LOW))
    sum_down.over_z()
    grad_branch, sum_down.total = barrier((grad_branch, sum_down.total))
    sum_down.share_y_nearest()
    grad_mixed = dot(out_weight, grad_branch, ((0,), (0,))).astype(LOW)

    grad_probs = dot(value_all, grad_mixed, ((0,), (0,)))
    grad_value_all = dot(grad_mixed, probs_low, ((1,), (1,)))
    grad_scores = (
        probs * (grad_probs - jnp.sum(probs * grad_probs, axis=0, keepdims=True))
    ).astype(LOW)
    grad_query_rot = dot(key_all, grad_scores, ((1,), (0,)))
    grad_key_all = dot(query_low, grad_scores, ((1,), (1,)))
    grad_kv_all = jnp.concatenate([grad_key_all, grad_value_all], axis=0)
    count = grad_kv_all.shape[1] // 2
    grad_kv_other = to_partner(grad_kv_all[:, count:].astype(LOW))
    grad_kv = grad_kv_all[:, :count] + grad_kv_other.astype(WIDE)
    grad_query, grad_g_query = query_pull(grad_query_rot)
    grad_key, grad_g_key = key_pull(grad_kv[:head])
    grad_query = grad_query.astype(LOW)
    grad_kv = jnp.concatenate([grad_key, grad_kv[head:]], axis=0).astype(LOW)
    grad_qkv = jnp.concatenate([grad_query, grad_kv], axis=0)

    grad_attn_part = dot(qkv_weight, grad_qkv, ((1,), (0,)))
    grad_attn_in = row_scatter(grad_attn_part)
    grad_g_in = jnp.sum(grad_attn_part * attn_in.astype(WIDE), axis=1) / gain_in[:, 0]

    head_gains = jnp.pad(
        jnp.stack([grad_g_query, grad_g_key], axis=1), ((0, features - head), (0, 0))
    )
    head_gains = mix(head_gains, head_gains)
    grad_gains = jnp.concatenate(
        [
            jnp.stack([grad_g_in, grad_g_post_attn, grad_g_pre_ffn, grad_g_post_ffn], axis=1),
            head_gains,
        ],
        axis=1,
    )
    slack = -grad_gains.shape[1] % 128
    gain_columns = jnp.pad(grad_gains, ((0, 0), (0, slack))).astype(LOW)

    def small_part(rows):
        return jnp.concatenate(
            [
                dot(attn_in[rows], grad_query, ((1,), (1,))).astype(LOW),
                dot(grad_branch[rows], mixed, ((1,), (1,))).astype(LOW),
                dot(attn_in[rows], grad_kv, ((1,), (1,))).astype(LOW),
                gain_columns[rows],
            ],
            axis=1,
        )

    sum_small = Small(small_part(slice(features, None)), small_part(slice(features)), place)
    sum_small.given, sum_down.near, sum_pair.total = barrier(
        (sum_small.given, sum_down.near, sum_pair.total)
    )
    sum_small.over_cores()
    sum_small.over_y_directly()
    sum_pair.over_z()
    sum_down.share_y_farthest()
    grad_attn_in, sum_pair.total = barrier((grad_attn_in, sum_pair.total))
    sum_pair.share_y_nearest()
    grad_in_norm, _ = norm_back(x, attn_factor, gain_in, grad_attn_in)
    grad_inputs, sum_small.total = barrier(
        ((grad_middle + grad_in_norm).astype(LOW), sum_small.total)
    )
    grad_inputs = back_together(grad_inputs)
    grad_inputs, sum_pair.near = barrier((grad_inputs, sum_pair.near))
    sum_pair.share_y_farthest()
    sum_small.over_z()
    sum_small.over_row(2 * head)
    sum_small.share_y()
    small = sum_small.share_cores()
    grad_w_down = sum_down.share_cores()
    grad_w_pair = sum_pair.share_cores()
    grad_w_gate, grad_w_up = grad_w_pair[:, :wide], grad_w_pair[:, wide:]
    grad_w_query, grad_w_out = small[:, :head], small[:, head : 2 * head]
    grad_w_key, grad_w_value = small[:, 2 * head : 3 * head], small[:, 3 * head : 4 * head]
    summed = small[:, 4 * head : 4 * head + 6].astype(WIDE).T

    whole = lambda w: w[:, :hidden_share].astype(WIDE)
    return (
        block_out.T[None],
        grad_inputs.T[None],
        grad_w_query.astype(WIDE),
        grad_w_key.astype(WIDE),
        grad_w_value.astype(WIDE),
        grad_w_out.astype(WIDE).T,
        whole(grad_w_gate),
        whole(grad_w_up),
        whole(grad_w_down).T,
        summed[0],
        summed[4, :head],
        summed[5, :head],
        summed[1],
        summed[2],
        summed[3],
    )


def solution(mesh):
    placed = (
        P("dp", "row", "col"),
        P("col", "row"),
        P("col", None),
        P("col", None),
        P("row", "col"),
        P("col", "row"),
        P("col", "row"),
        P("row", "col"),
        P("col"),
        P(),
        P(),
        P("col"),
        P("col"),
        P("col"),
        P("dp", "row", "col"),
    )
    return jax.shard_map(
        local,
        mesh=mesh,
        in_specs=placed,
        out_specs=(
            P("dp", "row", "col"),
            P("dp", "row", "col"),
            P("col", "row"),
            P("col", None),
            P("col", None),
            P("row", "col"),
            P("col", "row"),
            P("col", "row"),
            P("row", "col"),
            P("col"),
            P(),
            P(),
            P("col"),
            P("col"),
            P("col"),
        ),
        check_vma=False,
    )
```

```python
import jax
import jax.numpy as jnp
import numpy as np
from jax import lax
from jax.experimental import pallas as pl
from jax.experimental.pallas import tpu as pltpu
from jax.sharding import PartitionSpec as P

WINDOW = 512
EPSILON = 1e-06
MASKED = -1e30
ROPE_BASE = 10000.0
LOW = jnp.bfloat16
WIDE = jnp.float32

Y, HI, CORE, COL, ROW = 4, 2, 2, 2, 4


def device(y, z, core):
    return ((y * HI + z // COL) * CORE + core) * COL + z % COL


def z_route(shift_of):
    return [
        (device(y, z, core), device(y, (z + shift_of(z, core)) % 4, core))
        for y in range(Y)
        for z in range(4)
        for core in range(CORE)
    ]


def dp_route(target):
    return [(i, target(i)) for i in range(Y * HI * CORE)]


def by_z(shift_of):
    route = z_route(shift_of)
    return lambda v: lax.ppermute(v, ("dp", "col"), route)


to_partner = by_z(lambda z, core: 1 if z % 2 == 0 else -1)
to_cross = by_z(lambda z, core: -1 if z % 2 == 0 else 1)
to_opposite = by_z(lambda z, core: 2)
z_ring = by_z(lambda z, core: -1 if core == 0 else 1)


def core_swap(v):
    return lax.ppermute(v, "dp", dp_route(lambda i: i ^ 1))


def y_ring(v):
    step = HI * CORE
    return lax.ppermute(
        v, "dp", dp_route(lambda i: (i + (step if i % 2 == 0 else -step)) % (Y * step))
    )


def y_shift(v, distance):
    step = HI * CORE * distance
    return lax.ppermute(v, "dp", dp_route(lambda i: (i + step) % (Y * HI * CORE)))


def row_shift(v, distance):
    return lax.ppermute(v, "row", [(i, (i + distance) % ROW) for i in range(ROW)])


def row_gather(v):
    return jnp.concatenate([v, row_shift(v, 1), row_shift(v, -1), row_shift(v, 2)], axis=1)


def row_scatter_parts(total):
    share = total.shape[1] // ROW
    own, *others = [total[:, i * share : (i + 1) * share] for i in range(ROW)]
    return [own] + [
        row_shift(part.astype(LOW), distance)
        for part, distance in ((others[2], 2), (others[0], -1), (others[1], 1))
    ]


def row_scatter(total):
    own, *parts = row_scatter_parts(total)
    for part in parts:
        own = own + part.astype(WIDE)
    return own


def dot(left, right, dims):
    return lax.dot_general(left, right, (dims, ((), ())), preferred_element_type=WIDE)


def norm(v, gain):
    factor = lax.rsqrt(jnp.sum(v * v, axis=0, keepdims=True) / v.shape[0] + EPSILON)
    return v * factor * gain, factor


def norm_back(v, factor, gain, upstream):
    scaled = upstream * gain
    inner = jnp.sum(scaled * v, axis=0, keepdims=True)
    grad = factor * scaled - v * (factor * factor * factor) * inner / v.shape[0]
    return grad, jnp.sum(upstream * v * factor, axis=1)


def head_map(raw, gain, cosine, sine, scaling):
    normed = (
        raw * lax.rsqrt(jnp.mean(raw * raw, axis=0, keepdims=True) + EPSILON) * gain[:, None]
    )
    half = raw.shape[0] // 2
    first, second = normed[:half], normed[half:]
    turned = jnp.concatenate(
        [first * cosine - second * sine, second * cosine + first * sine], axis=0
    )
    return turned * scaling


def geglu(gate, up):
    return jax.nn.gelu(gate, approximate=True) * up


def rope_tables(length, head_size):
    half = head_size // 2
    exponent = np.arange(half, dtype=np.float32) * np.float32(2.0 / head_size)
    rate = np.float32(ROPE_BASE) ** (-exponent)
    angles = rate[:, None] * np.arange(length, dtype=np.float32)[None, :]
    return np.stack([np.cos(angles), np.sin(angles)]).astype(np.float32)


def pick(v, index, axis):
    return lax.dynamic_index_in_dim(v, index, axis, keepdims=False)


def pack_kernel(core, weight, packed):
    packed[...] = weight[...]


def pack(core, weight):
    block = (weight.shape[0] // 2, weight.shape[1])
    return pl.pallas_call(
        pack_kernel,
        grid_spec=pltpu.PrefetchScalarGridSpec(
            num_scalar_prefetch=1,
            grid=(1,),
            in_specs=[pl.BlockSpec(block, lambda i, core: (core[0], 0))],
            out_specs=pl.BlockSpec(block, lambda i, core: (0, 0)),
        ),
        out_shape=jax.ShapeDtypeStruct(block, weight.dtype),
        compiler_params=pltpu.CompilerParams(vmem_limit_bytes=16 * 2**20),
        cost_estimate=pl.CostEstimate(
            flops=0, bytes_accessed=4 * block[0] * block[1], transcendentals=0
        ),
    )(core.reshape(1), weight)


def join_kernel(count, core, *refs):
    owns, mine, theirs, wholes = [refs[i * count : (i + 1) * count] for i in range(4)]
    step = pl.program_id(0)
    for i in range(count):

        @pl.when(step % 2 == 0)
        def _():
            wholes[i][...] = owns[i][...]

        @pl.when(step == 1)
        def _():
            wholes[i][...] = mine[i][...]

        @pl.when(step == 3)
        def _():
            wholes[i][...] = theirs[i][...]


def join(core, owns, mine, theirs):
    count = len(owns)
    block = (owns[0].shape[0] // 2, owns[0].shape[1])
    part = pl.BlockSpec(block, lambda i, core: (0, 0))
    own = pl.BlockSpec(block, lambda i, core: (jnp.where(i < 2, core[0], 1 - core[0]), 0))
    return pl.pallas_call(
        lambda *refs: join_kernel(count, *refs),
        grid_spec=pltpu.PrefetchScalarGridSpec(
            num_scalar_prefetch=1,
            grid=(4,),
            in_specs=[own] * count + [part] * (2 * count),
            out_specs=[pl.BlockSpec(block, lambda i, core: (i, 0))] * count,
        ),
        out_shape=[jax.ShapeDtypeStruct((4 * block[0], block[1]), owns[0].dtype)] * count,
        compiler_params=pltpu.CompilerParams(vmem_limit_bytes=40 * 2**20),
        cost_estimate=pl.CostEstimate(
            flops=0, bytes_accessed=16 * count * block[0] * block[1], transcendentals=0
        ),
    )(core.reshape(1), *owns, *mine, *theirs)


def add(a, b):
    return (a.astype(WIDE) + b.astype(WIDE)).astype(LOW)


Y_GROUPS = [[y * HI * CORE + i for y in range(Y)] for i in range(HI * CORE)]


class Sum:
    def __init__(self, left, right, place):
        self.y, self.z, self.core = place
        rows, self.width = left.shape[0] // 2, right.shape[0]
        product = lambda part: dot(part, right, ((1,), (1,))).astype(LOW)
        self.given, self.kept = product(left[rows:]), product(left[:rows])

    def over_cores(self):
        held = add(self.kept, core_swap(self.given))
        self.held = held.reshape(COL, Y, -1, self.width).swapaxes(0, 1)

    def over_y(self):
        self.total = lax.psum_scatter(
            self.held.reshape(-1, self.width),
            "dp",
            scatter_dimension=0,
            axis_index_groups=Y_GROUPS,
            tiled=True,
        ).reshape(COL, -1, self.width)

    def over_y_directly(self):
        chunk = lambda distance: pick(self.held, (self.y + distance) % Y, 0)
        total = chunk(0).astype(WIDE)
        for distance in (2, 1, 3):
            total = total + y_shift(chunk(distance), distance).astype(WIDE)
        self.total = total.astype(LOW)

    def over_z(self):
        total = add(self.total[0], to_partner(self.total[1]))
        self.total = add(total, to_opposite(total))

    def over_row(self, start):
        sent = self.total[:, start:]
        part = sent.astype(WIDE)
        for distance in (2, 1, 3):
            part = part + row_shift(sent, distance).astype(WIDE)
        self.total = jnp.concatenate([self.total[:, :start], part.astype(LOW)], axis=1)

    def share_y_nearest(self):
        self.near = y_shift(self.total, 1), y_shift(self.total, -1)

    def share_y_farthest(self):
        below, above = self.near
        half = self.width // 2
        across = jnp.concatenate(
            [y_shift(below[:, :half], 1), y_shift(above[:, half:], -1)], axis=1
        )
        self.lay_y(self.total, below, across, above)

    def share_y(self):
        self.lay_y(self.total, *[y_shift(self.total, distance) for distance in (1, 2, 3)])

    def lay_y(self, *parts):
        ring = jnp.stack(parts)
        self.mine = jnp.concatenate([pick(ring, (self.y - j) % Y, 0) for j in range(Y)], axis=0)

    def share_cores(self, *before):
        theirs = core_swap(self.mine)
        if before:
            theirs, *before = lax.optimization_barrier((theirs, *before))
        first = jnp.where(self.core == 0, self.mine, theirs)
        second = jnp.where(self.core == 0, theirs, self.mine)
        both = jnp.concatenate([first, second], axis=0)
        return (both, *before) if before else both


class Small(Sum):
    def __init__(self, given, kept, place):
        self.y, self.z, self.core = place
        self.given, self.kept, self.width = given, kept, given.shape[1]


class Shared(Sum):
    def __init__(self, sums, place):
        self.y, self.z, self.core = place
        self.total = jnp.concatenate([part.total for part in sums], axis=1)
        self.width = self.total.shape[1]


def local(
    inputs,
    w_query,
    w_key,
    w_value,
    attention_output_weight,
    w_gate,
    w_up,
    down_weight,
    g_in,
    g_query,
    g_key,
    g_post_attn,
    g_pre_ffn,
    g_post_ffn,
    cotangent,
):
    col, row, dp = lax.axis_index("col"), lax.axis_index("row"), lax.axis_index("dp")
    core, hi, y = dp % CORE, (dp // CORE) % HI, dp // (HI * CORE)
    place = (y, hi * COL + col, core)
    features, share = inputs.shape[2], inputs.shape[1] // COL
    head = g_query.shape[0]
    hidden_share = w_gate.shape[1]
    wide = hidden_share + -hidden_share % 256
    barrier = lax.optimization_barrier

    def mix(own, other):
        half = own.shape[0] // 2
        parts = [v[:half] for v in (own, other)], [v[half:] for v in (own, other)]
        first = [jnp.where(core == 0, a, b) for a, b in zip(*parts)]
        second = [jnp.where(core == 0, b, a) for a, b in zip(*parts)]
        return jnp.concatenate(first + second, axis=0)

    def unmix(v):
        half = v.shape[0] // 4
        own_a, other_a, own_b, other_b = [v[i * half : (i + 1) * half] for i in range(4)]
        lay = lambda a, b: jnp.concatenate(
            [jnp.where(core == 0, a, b), jnp.where(core == 0, b, a)], axis=0
        )
        return lay(own_a, own_b), lay(other_a, other_b)

    def spread(v):
        kept = lax.dynamic_slice_in_dim(v, col * share, share, 1)
        given = lax.dynamic_slice_in_dim(v, (1 - col) * share, share, 1)
        return kept, to_partner(given)

    def back_together(*values):
        pairs = [unmix(v) for v in values]
        theirs = to_partner(jnp.concatenate([given for _, given in pairs], axis=0))
        received = [theirs[i * features : (i + 1) * features] for i in range(len(pairs))]
        return [
            jnp.where(
                col == 0,
                jnp.concatenate([kept, other], axis=1),
                jnp.concatenate([other, kept], axis=1),
            )
            for (kept, _), other in zip(pairs, received)
        ]

    kept, taken = spread(inputs[0].T)
    gains_own = jnp.stack([g_in, g_post_attn, g_pre_ffn, g_post_ffn])
    gains_other = to_partner(gains_own)
    gains = mix(gains_own.T, gains_other.T)
    gain_in, gain_post_attn, gain_pre_ffn, gain_post_ffn = [gains[:, i : i + 1] for i in range(4)]

    x = mix(kept, taken).astype(WIDE)
    attn_norm, attn_factor = norm(x, gain_in)
    attn_norm, w_query, w_gate = barrier((attn_norm.astype(LOW), w_query, w_gate))
    attn_in = row_gather(attn_norm)

    attn_own = jnp.concatenate([w_query, w_key, w_value, attention_output_weight.T], axis=1)
    attn_mine = z_ring(pack(core, attn_own))
    gate_mine = z_ring(pack(core, w_gate))
    up_sent, gate_mine = barrier((pack(core, w_up), gate_mine))
    up_mine = z_ring(up_sent)
    (attn_weight,) = join(core, [attn_own], [attn_mine], [core_swap(attn_mine)])
    qkv_weight, out_weight = attn_weight[:, : 3 * head], attn_weight[:, 3 * head :]

    qkv = dot(qkv_weight, attn_in, ((0,), (0,)))
    raw_query, raw_key, value = qkv[:head], qkv[head : 2 * head], qkv[2 * head :].astype(LOW)

    chunk_rows = [row, (row - 1) % ROW, (row + 1) % ROW, (row + 2) % ROW]
    tables = jnp.asarray(rope_tables(ROW * COL * share, head))
    turns = jnp.concatenate(
        [
            lax.dynamic_slice_in_dim(tables, (r * COL + col) * share, share, 2)
            for r in chunk_rows
        ],
        axis=2,
    )
    cosine, sine = turns[0], turns[1]
    query_rot, query_pull = jax.vjp(
        lambda v, g: head_map(v, g, cosine, sine, head**-0.5), raw_query, g_query
    )
    key_rot, key_pull = jax.vjp(lambda v, g: head_map(v, g, cosine, sine, 1.0), raw_key, g_key)
    query_low = query_rot.astype(LOW)
    key_value = jnp.concatenate([key_rot.astype(LOW), value], axis=0)
    key_value_other, down_sent = barrier((to_partner(key_value), pack(core, down_weight.T)))
    down_mine = z_ring(down_sent)
    key_value = jnp.concatenate([key_value, key_value_other], axis=1)
    key_all, value_all = key_value[:head], key_value[head:]

    steps = np.repeat(np.array([0, -1, 1, 2], np.int32), share)
    within = np.tile(np.arange(share, dtype=np.int32), ROW)
    position = lambda c: (((row + steps) % ROW) * COL + c) * share + within
    query_position = position(col)
    key_position = jnp.concatenate([query_position, position(1 - col)])
    offset = query_position[None, :] - key_position[:, None]
    allowed = (offset >= 0) & (offset < WINDOW)
    scores = jnp.where(allowed, dot(key_all, query_low, ((0,), (0,))), MASKED)
    weights = jnp.exp(scores - jnp.max(scores, axis=0, keepdims=True))
    probs = weights / jnp.sum(weights, axis=0, keepdims=True)
    probs_low = probs.astype(LOW)
    mixed = dot(value_all, probs_low, ((1,), (0,))).astype(LOW)
    branch_part = dot(out_weight, mixed, ((1,), (0,)))
    branch = row_scatter(branch_part)
    pair_mine = [gate_mine, up_mine]
    gate_weight, up_weight = join(
        core, [w_gate, w_up], pair_mine, [core_swap(part) for part in pair_mine]
    )
    down_mine, branch = barrier((down_mine, branch))
    (down_t,) = join(core, [down_weight.T], [down_mine], [core_swap(down_mine)])
    post_attn, post_factor = norm(branch, gain_post_attn)
    middle = x + post_attn
    ffn_norm, ffn_factor = norm(middle, gain_pre_ffn)
    ffn_in = row_gather(ffn_norm.astype(LOW))

    gate = dot(gate_weight, ffn_in, ((0,), (0,)))
    up = dot(up_weight, ffn_in, ((0,), (0,)))
    hidden, geglu_pull = jax.vjp(geglu, gate, up)
    hidden = hidden.astype(LOW)
    down_proj = row_scatter(dot(down_t, hidden, ((1,), (0,))))
    post_ffn, post_ffn_factor = norm(down_proj, gain_post_ffn)
    block_out = (middle + post_ffn).astype(LOW)

    kept, taken = spread(cotangent[0].T)
    upstream = mix(kept, taken).astype(WIDE)
    grad_down, grad_g_post_ffn = norm_back(down_proj, post_ffn_factor, gain_post_ffn, upstream)
    grad_down = row_gather(grad_down.astype(LOW))
    more = lambda v: jnp.pad(v, ((0, wide - hidden_share), (0, 0)))
    sum_down = Sum(grad_down, more(hidden), place)
    sum_down.given, grad_down = barrier((sum_down.given, grad_down))
    sum_down.over_cores()
    sum_down.over_y()
    grad_gate, grad_up = geglu_pull(dot(down_t, grad_down, ((0,), (0,))))
    grad_gate, grad_up = grad_gate.astype(LOW), grad_up.astype(LOW)
    grad_pair = jnp.concatenate([more(grad_gate), more(grad_up)], axis=0)
    grad_pair, grad_gate, grad_up = barrier((grad_pair, grad_gate, grad_up))
    sum_pair = Sum(ffn_in, grad_pair, place)
    sum_pair.given, grad_gate, grad_up = barrier((sum_pair.given, grad_gate, grad_up))
    sum_pair.over_cores()
    own, far, left, right = row_scatter_parts(
        dot(gate_weight, grad_gate, ((1,), (0,))) + dot(up_weight, grad_up, ((1,), (0,)))
    )
    own, sum_pair.held = barrier((own, sum_pair.held))
    sum_pair.over_y()
    grad_ffn_in = own + left.astype(WIDE) + right.astype(WIDE) + far.astype(WIDE)

    grad_mid_norm, grad_g_pre_ffn = norm_back(middle, ffn_factor, gain_pre_ffn, grad_ffn_in)
    grad_middle = upstream + grad_mid_norm
    grad_branch, grad_g_post_attn = norm_back(branch, post_factor, gain_post_attn, grad_middle)
    grad_branch = row_gather(grad_branch.astype(LOW))
    sum_down.over_z()
    grad_branch, sum_down.total = barrier((grad_branch, sum_down.total))
    grad_mixed = dot(out_weight, grad_branch, ((0,), (0,))).astype(LOW)

    grad_probs = dot(value_all, grad_mixed, ((0,), (0,)))
    grad_value_all = dot(grad_mixed, probs_low, ((1,), (1,)))
    grad_scores = (
        probs * (grad_probs - jnp.sum(probs * grad_probs, axis=0, keepdims=True))
    ).astype(LOW)
    grad_query_rot = dot(key_all, grad_scores, ((1,), (0,)))
    grad_key_all = dot(query_low, grad_scores, ((1,), (1,)))
    grad_kv_all = jnp.concatenate([grad_key_all, grad_value_all], axis=0)
    count = grad_kv_all.shape[1] // 2
    grad_kv_other = to_partner(grad_kv_all[:, count:].astype(LOW))
    grad_kv = grad_kv_all[:, :count] + grad_kv_other.astype(WIDE)
    grad_query, grad_g_query = query_pull(grad_query_rot)
    grad_key, grad_g_key = key_pull(grad_kv[:head])
    grad_query = grad_query.astype(LOW)
    grad_kv = jnp.concatenate([grad_key, grad_kv[head:]], axis=0).astype(LOW)
    grad_qkv = jnp.concatenate([grad_query, grad_kv], axis=0)

    grad_attn_part = dot(qkv_weight, grad_qkv, ((1,), (0,)))
    grad_g_in = jnp.sum(grad_attn_part * attn_in.astype(WIDE), axis=1) / gain_in[:, 0]

    head_gains = jnp.pad(
        jnp.stack([grad_g_query, grad_g_key], axis=1), ((0, features - head), (0, 0))
    )
    head_gains = mix(head_gains, head_gains)
    grad_gains = jnp.concatenate(
        [
            jnp.stack([grad_g_in, grad_g_post_attn, grad_g_pre_ffn, grad_g_post_ffn], axis=1),
            head_gains,
        ],
        axis=1,
    )
    slack = -grad_gains.shape[1] % 128
    gain_columns = jnp.pad(grad_gains, ((0, 0), (0, slack))).astype(LOW)

    def small_part(rows):
        return jnp.concatenate(
            [
                dot(attn_in[rows], grad_query, ((1,), (1,))).astype(LOW),
                dot(grad_branch[rows], mixed, ((1,), (1,))).astype(LOW),
                dot(attn_in[rows], grad_kv, ((1,), (1,))).astype(LOW),
                gain_columns[rows],
            ],
            axis=1,
        )

    sum_small = Small(small_part(slice(features, None)), small_part(slice(features)), place)
    sum_small.given, grad_attn_part, sum_pair.total = barrier(
        (sum_small.given, grad_attn_part, sum_pair.total)
    )
    sum_small.over_cores()
    sum_pair.over_z()
    grad_attn_in = row_scatter(grad_attn_part)
    sum_small.over_y_directly()
    grad_in_norm, _ = norm_back(x, attn_factor, gain_in, grad_attn_in)
    grad_inputs = (grad_middle + grad_in_norm).astype(LOW)
    sum_small.total, sum_pair.total, grad_inputs = barrier(
        (sum_small.total, sum_pair.total, grad_inputs)
    )
    block_out, grad_inputs = back_together(block_out, grad_inputs)
    shared = Shared([sum_pair, sum_down], place)
    shared.share_y_nearest()
    sum_small.over_z()
    sum_small.total, shared.near = barrier((sum_small.total, shared.near))
    shared.share_y_farthest()
    sum_small.over_row(2 * head)
    sum_small.total, shared.mine, block_out, grad_inputs = barrier(
        (sum_small.total, shared.mine, block_out, grad_inputs)
    )
    sum_small.share_y()
    grad_w_all = shared.share_cores()
    columns = lambda start, count: grad_w_all[:, start : start + count]
    small, grad_w_gate, grad_w_up, grad_w_down = sum_small.share_cores(
        *[columns(i * wide, hidden_share).astype(WIDE) for i in range(3)]
    )
    grad_w_query, grad_w_out = small[:, :head], small[:, head : 2 * head]
    grad_w_key, grad_w_value = small[:, 2 * head : 3 * head], small[:, 3 * head : 4 * head]
    summed = small[:, 4 * head : 4 * head + 6].astype(WIDE).T

    return (
        block_out.T[None],
        grad_inputs.T[None],
        grad_w_query.astype(WIDE),
        grad_w_key.astype(WIDE),
        grad_w_value.astype(WIDE),
        grad_w_out.astype(WIDE).T,
        grad_w_gate,
        grad_w_up,
        grad_w_down.T,
        summed[0],
        summed[4, :head],
        summed[5, :head],
        summed[1],
        summed[2],
        summed[3],
    )


def solution(mesh):
    placed = (
        P("dp", "row", "col"),
        P("col", "row"),
        P("col", None),
        P("col", None),
        P("row", "col"),
        P("col", "row"),
        P("col", "row"),
        P("row", "col"),
        P("col"),
        P(),
        P(),
        P("col"),
        P("col"),
        P("col"),
        P("dp", "row", "col"),
    )
    return jax.shard_map(
        local,
        mesh=mesh,
        in_specs=placed,
        out_specs=(
            P("dp", "row", "col"),
            P("dp", "row", "col"),
            P("col", "row"),
            P("col", None),
            P("col", None),
            P("row", "col"),
            P("col", "row"),
            P("col", "row"),
            P("row", "col"),
            P("col"),
            P(),
            P(),
            P("col"),
            P("col"),
            P("col"),
        ),
        check_vma=False,
    )
```

```python
import jax
import jax.numpy as jnp
import numpy as np
from jax import lax
from jax.experimental import pallas as pl
from jax.experimental.pallas import tpu as pltpu
from jax.sharding import PartitionSpec as P

WINDOW = 512
EPSILON = 1e-06
MASKED = -1e30
ROPE_BASE = 10000.0
LOW = jnp.bfloat16
WIDE = jnp.float32

Y, HI, CORE, COL, ROW = 4, 2, 2, 2, 4


def device(y, z, core):
    return ((y * HI + z // COL) * CORE + core) * COL + z % COL


def z_route(shift_of):
    return [
        (device(y, z, core), device(y, (z + shift_of(z, core)) % 4, core))
        for y in range(Y)
        for z in range(4)
        for core in range(CORE)
    ]


def dp_route(target):
    return [(i, target(i)) for i in range(Y * HI * CORE)]


def by_z(shift_of):
    route = z_route(shift_of)
    return lambda v: lax.ppermute(v, ("dp", "col"), route)


to_partner = by_z(lambda z, core: 1 if z % 2 == 0 else -1)
to_cross = by_z(lambda z, core: -1 if z % 2 == 0 else 1)
to_opposite = by_z(lambda z, core: 2)
z_ring = by_z(lambda z, core: -1 if core == 0 else 1)


def core_swap(v):
    return lax.ppermute(v, "dp", dp_route(lambda i: i ^ 1))


def y_ring(v):
    step = HI * CORE
    return lax.ppermute(
        v, "dp", dp_route(lambda i: (i + (step if i % 2 == 0 else -step)) % (Y * step))
    )


def y_shift(v, distance):
    step = HI * CORE * distance
    return lax.ppermute(v, "dp", dp_route(lambda i: (i + step) % (Y * HI * CORE)))


def row_shift(v, distance):
    return lax.ppermute(v, "row", [(i, (i + distance) % ROW) for i in range(ROW)])


def row_gather(v):
    return jnp.concatenate([v, row_shift(v, 1), row_shift(v, -1), row_shift(v, 2)], axis=1)


def row_chunks(total):
    share = total.shape[1] // ROW
    own, *others = [total[:, i * share : (i + 1) * share] for i in range(ROW)]
    return [own] + [others[i].astype(LOW) for i in (2, 0, 1)]


def send_chunks(own, *sent):
    return [own] + [row_shift(part, distance) for part, distance in zip(sent, (2, -1, 1))]


def row_scatter_parts(total):
    return send_chunks(*row_chunks(total))


def row_scatter(total):
    own, *parts = row_scatter_parts(total)
    for part in parts:
        own = own + part.astype(WIDE)
    return own


def dot(left, right, dims):
    return lax.dot_general(left, right, (dims, ((), ())), preferred_element_type=WIDE)


def norm(v, gain):
    factor = lax.rsqrt(jnp.sum(v * v, axis=0, keepdims=True) / v.shape[0] + EPSILON)
    return v * factor * gain, factor


def norm_back(v, factor, gain, upstream):
    scaled = upstream * gain
    inner = jnp.sum(scaled * v, axis=0, keepdims=True)
    grad = factor * scaled - v * (factor * factor * factor) * inner / v.shape[0]
    return grad, jnp.sum(upstream * v * factor, axis=1)


def head_map(raw, gain, cosine, sine, scaling):
    normed = (
        raw * lax.rsqrt(jnp.mean(raw * raw, axis=0, keepdims=True) + EPSILON) * gain[:, None]
    )
    half = raw.shape[0] // 2
    first, second = normed[:half], normed[half:]
    turned = jnp.concatenate(
        [first * cosine - second * sine, second * cosine + first * sine], axis=0
    )
    return turned * scaling


def geglu(gate, up):
    return jax.nn.gelu(gate, approximate=True) * up


def rope_tables(length, head_size):
    half = head_size // 2
    exponent = np.arange(half, dtype=np.float32) * np.float32(2.0 / head_size)
    rate = np.float32(ROPE_BASE) ** (-exponent)
    angles = rate[:, None] * np.arange(length, dtype=np.float32)[None, :]
    return np.stack([np.cos(angles), np.sin(angles)]).astype(np.float32)


def pick(v, index, axis):
    return lax.dynamic_index_in_dim(v, index, axis, keepdims=False)


def pack_kernel(core, weight, packed):
    packed[...] = weight[...]


def pack(core, weight):
    block = (weight.shape[0] // 2, weight.shape[1])
    return pl.pallas_call(
        pack_kernel,
        grid_spec=pltpu.PrefetchScalarGridSpec(
            num_scalar_prefetch=1,
            grid=(1,),
            in_specs=[pl.BlockSpec(block, lambda i, core: (core[0], 0))],
            out_specs=pl.BlockSpec(block, lambda i, core: (0, 0)),
        ),
        out_shape=jax.ShapeDtypeStruct(block, weight.dtype),
        compiler_params=pltpu.CompilerParams(vmem_limit_bytes=16 * 2**20),
        cost_estimate=pl.CostEstimate(
            flops=0, bytes_accessed=4 * block[0] * block[1], transcendentals=0
        ),
    )(core.reshape(1), weight)


def join_kernel(count, core, *refs):
    owns, mine, theirs, wholes = [refs[i * count : (i + 1) * count] for i in range(4)]
    step = pl.program_id(0)
    for i in range(count):

        @pl.when(step % 2 == 0)
        def _():
            wholes[i][...] = owns[i][...]

        @pl.when(step == 1)
        def _():
            wholes[i][...] = mine[i][...]

        @pl.when(step == 3)
        def _():
            wholes[i][...] = theirs[i][...]


def join(core, owns, mine, theirs):
    count = len(owns)
    block = (owns[0].shape[0] // 2, owns[0].shape[1])
    part = pl.BlockSpec(block, lambda i, core: (0, 0))
    own = pl.BlockSpec(block, lambda i, core: (jnp.where(i < 2, core[0], 1 - core[0]), 0))
    return pl.pallas_call(
        lambda *refs: join_kernel(count, *refs),
        grid_spec=pltpu.PrefetchScalarGridSpec(
            num_scalar_prefetch=1,
            grid=(4,),
            in_specs=[own] * count + [part] * (2 * count),
            out_specs=[pl.BlockSpec(block, lambda i, core: (i, 0))] * count,
        ),
        out_shape=[jax.ShapeDtypeStruct((4 * block[0], block[1]), owns[0].dtype)] * count,
        compiler_params=pltpu.CompilerParams(vmem_limit_bytes=40 * 2**20),
        cost_estimate=pl.CostEstimate(
            flops=0, bytes_accessed=16 * count * block[0] * block[1], transcendentals=0
        ),
    )(core.reshape(1), *owns, *mine, *theirs)


def add(a, b):
    return (a.astype(WIDE) + b.astype(WIDE)).astype(LOW)


Y_GROUPS = [[y * HI * CORE + i for y in range(Y)] for i in range(HI * CORE)]


class Sum:
    def __init__(self, left, right, place):
        self.y, self.z, self.core = place
        rows, self.width = left.shape[0] // 2, right.shape[0]
        product = lambda part: dot(part, right, ((1,), (1,))).astype(LOW)
        self.given, self.kept = product(left[rows:]), product(left[:rows])

    def over_cores(self):
        held = add(self.kept, core_swap(self.given))
        self.held = held.reshape(COL, Y, -1, self.width).swapaxes(0, 1)

    def over_y(self):
        self.total = lax.psum_scatter(
            self.held.reshape(-1, self.width),
            "dp",
            scatter_dimension=0,
            axis_index_groups=Y_GROUPS,
            tiled=True,
        ).reshape(COL, -1, self.width)

    def over_y_directly(self):
        chunk = lambda distance: pick(self.held, (self.y + distance) % Y, 0)
        total = chunk(0).astype(WIDE)
        for distance in (2, 1, 3):
            total = total + y_shift(chunk(distance), distance).astype(WIDE)
        self.total = total.astype(LOW)

    def over_z(self):
        self.over_col()
        self.over_hi()

    def over_col(self):
        self.total = add(self.total[0], to_partner(self.total[1]))

    def over_hi(self):
        self.total = add(self.total, to_opposite(self.total))

    def over_row(self, start):
        sent = self.total[:, start:]
        part = sent.astype(WIDE)
        for distance in (2, 1, 3):
            part = part + row_shift(sent, distance).astype(WIDE)
        self.total = jnp.concatenate([self.total[:, :start], part.astype(LOW)], axis=1)

    def share_y_nearest(self):
        self.near = y_shift(self.total, 1), y_shift(self.total, -1)

    def share_y_farthest(self):
        below, above = self.near
        half = self.width // 2
        self.across = jnp.concatenate(
            [y_shift(below[:, :half], 1), y_shift(above[:, half:], -1)], axis=1
        )
        self.other_near = core_swap(jnp.concatenate([self.total, below, above], axis=0))

    def share_cores_last(self):
        rows = self.total.shape[0]
        below, above = self.near
        other = [self.other_near[i * rows : (i + 1) * rows] for i in range(3)]
        self.lay_y(self.total, below, self.across, above)
        mine = self.mine
        self.lay_y(other[0], other[1], core_swap(self.across), other[2])
        theirs = self.mine
        first = jnp.where(self.core == 0, mine, theirs)
        second = jnp.where(self.core == 0, theirs, mine)
        return jnp.concatenate([first, second], axis=0)

    def share_y(self):
        self.lay_y(self.total, *[y_shift(self.total, distance) for distance in (1, 2, 3)])

    def lay_y(self, *parts):
        ring = jnp.stack(parts)
        self.mine = jnp.concatenate([pick(ring, (self.y - j) % Y, 0) for j in range(Y)], axis=0)

    def share_cores(self, *before):
        theirs = core_swap(self.mine)
        if before:
            theirs, *before = lax.optimization_barrier((theirs, *before))
        first = jnp.where(self.core == 0, self.mine, theirs)
        second = jnp.where(self.core == 0, theirs, self.mine)
        both = jnp.concatenate([first, second], axis=0)
        return (both, *before) if before else both


class Small(Sum):
    def __init__(self, given, kept, place):
        self.y, self.z, self.core = place
        self.given, self.kept, self.width = given, kept, given.shape[1]


class Shared(Sum):
    def __init__(self, sums, place):
        self.y, self.z, self.core = place
        self.total = jnp.concatenate([part.total for part in sums], axis=1)
        self.width = self.total.shape[1]


def local(
    inputs,
    w_query,
    w_key,
    w_value,
    attention_output_weight,
    w_gate,
    w_up,
    down_weight,
    g_in,
    g_query,
    g_key,
    g_post_attn,
    g_pre_ffn,
    g_post_ffn,
    cotangent,
):
    col, row, dp = lax.axis_index("col"), lax.axis_index("row"), lax.axis_index("dp")
    core, hi, y = dp % CORE, (dp // CORE) % HI, dp // (HI * CORE)
    place = (y, hi * COL + col, core)
    features, share = inputs.shape[2], inputs.shape[1] // COL
    head = g_query.shape[0]
    hidden_share = w_gate.shape[1]
    wide = hidden_share + -hidden_share % 256
    barrier = lax.optimization_barrier

    def mix(own, other):
        half = own.shape[0] // 2
        parts = [v[:half] for v in (own, other)], [v[half:] for v in (own, other)]
        first = [jnp.where(core == 0, a, b) for a, b in zip(*parts)]
        second = [jnp.where(core == 0, b, a) for a, b in zip(*parts)]
        return jnp.concatenate(first + second, axis=0)

    def unmix(v):
        half = v.shape[0] // 4
        own_a, other_a, own_b, other_b = [v[i * half : (i + 1) * half] for i in range(4)]
        lay = lambda a, b: jnp.concatenate(
            [jnp.where(core == 0, a, b), jnp.where(core == 0, b, a)], axis=0
        )
        return lay(own_a, own_b), lay(other_a, other_b)

    def spread(v):
        kept = lax.dynamic_slice_in_dim(v, col * share, share, 1)
        given = lax.dynamic_slice_in_dim(v, (1 - col) * share, share, 1)
        return kept, to_partner(given)

    def back_together(*values):
        pairs = [unmix(v) for v in values]
        theirs = to_partner(jnp.concatenate([given for _, given in pairs], axis=0))
        received = [theirs[i * features : (i + 1) * features] for i in range(len(pairs))]
        return [
            jnp.where(
                col == 0,
                jnp.concatenate([kept, other], axis=1),
                jnp.concatenate([other, kept], axis=1),
            )
            for (kept, _), other in zip(pairs, received)
        ]

    kept, taken = spread(inputs[0].T)
    gains_own = jnp.stack([g_in, g_post_attn, g_pre_ffn, g_post_ffn])
    gains_other = to_partner(gains_own)
    gains = mix(gains_own.T, gains_other.T)
    gain_in, gain_post_attn, gain_pre_ffn, gain_post_ffn = [gains[:, i : i + 1] for i in range(4)]

    x = mix(kept, taken).astype(WIDE)
    attn_norm, attn_factor = norm(x, gain_in)
    attn_norm, w_query, w_gate = barrier((attn_norm.astype(LOW), w_query, w_gate))
    attn_in = row_gather(attn_norm)

    attn_own = jnp.concatenate([w_query, w_key, w_value, attention_output_weight.T], axis=1)
    attn_mine = z_ring(pack(core, attn_own))
    gate_mine = z_ring(pack(core, w_gate))
    up_sent, gate_mine = barrier((pack(core, w_up), gate_mine))
    up_mine = z_ring(up_sent)
    (attn_weight,) = join(core, [attn_own], [attn_mine], [core_swap(attn_mine)])
    qkv_weight, out_weight = attn_weight[:, : 3 * head], attn_weight[:, 3 * head :]

    qkv = dot(qkv_weight, attn_in, ((0,), (0,)))
    raw_query, raw_key, value = qkv[:head], qkv[head : 2 * head], qkv[2 * head :].astype(LOW)

    chunk_rows = [row, (row - 1) % ROW, (row + 1) % ROW, (row + 2) % ROW]
    tables = jnp.asarray(rope_tables(ROW * COL * share, head))
    turns = jnp.concatenate(
        [
            lax.dynamic_slice_in_dim(tables, (r * COL + col) * share, share, 2)
            for r in chunk_rows
        ],
        axis=2,
    )
    cosine, sine = turns[0], turns[1]
    query_rot, query_pull = jax.vjp(
        lambda v, g: head_map(v, g, cosine, sine, head**-0.5), raw_query, g_query
    )
    key_rot, key_pull = jax.vjp(lambda v, g: head_map(v, g, cosine, sine, 1.0), raw_key, g_key)
    query_low = query_rot.astype(LOW)
    key_value = jnp.concatenate([key_rot.astype(LOW), value], axis=0)
    key_value_other, down_sent = barrier((to_partner(key_value), pack(core, down_weight.T)))
    down_mine = z_ring(down_sent)
    key_value = jnp.concatenate([key_value, key_value_other], axis=1)
    key_all, value_all = key_value[:head], key_value[head:]

    steps = np.repeat(np.array([0, -1, 1, 2], np.int32), share)
    within = np.tile(np.arange(share, dtype=np.int32), ROW)
    position = lambda c: (((row + steps) % ROW) * COL + c) * share + within
    query_position = position(col)
    key_position = jnp.concatenate([query_position, position(1 - col)])
    offset = query_position[None, :] - key_position[:, None]
    allowed = (offset >= 0) & (offset < WINDOW)
    scores = jnp.where(allowed, dot(key_all, query_low, ((0,), (0,))), MASKED)
    weights = jnp.exp(scores - jnp.max(scores, axis=0, keepdims=True))
    probs = weights / jnp.sum(weights, axis=0, keepdims=True)
    probs_low = probs.astype(LOW)
    mixed = dot(value_all, probs_low, ((1,), (0,))).astype(LOW)
    branch_part = dot(out_weight, mixed, ((1,), (0,)))
    branch = row_scatter(branch_part)
    pair_mine = [gate_mine, up_mine]
    gate_weight, up_weight = join(
        core, [w_gate, w_up], pair_mine, [core_swap(part) for part in pair_mine]
    )
    down_mine, branch = barrier((down_mine, branch))
    (down_t,) = join(core, [down_weight.T], [down_mine], [core_swap(down_mine)])
    post_attn, post_factor = norm(branch, gain_post_attn)
    middle = x + post_attn
    ffn_norm, ffn_factor = norm(middle, gain_pre_ffn)
    ffn_in = row_gather(ffn_norm.astype(LOW))

    gate = dot(gate_weight, ffn_in, ((0,), (0,)))
    up = dot(up_weight, ffn_in, ((0,), (0,)))
    hidden, geglu_pull = jax.vjp(geglu, gate, up)
    hidden = hidden.astype(LOW)
    down_proj = row_scatter(dot(down_t, hidden, ((1,), (0,))))
    post_ffn, post_ffn_factor = norm(down_proj, gain_post_ffn)
    block_out = (middle + post_ffn).astype(LOW)

    kept, taken = spread(cotangent[0].T)
    upstream = mix(kept, taken).astype(WIDE)
    grad_down, grad_g_post_ffn = norm_back(down_proj, post_ffn_factor, gain_post_ffn, upstream)
    grad_down = row_gather(grad_down.astype(LOW))
    more = lambda v: jnp.pad(v, ((0, wide - hidden_share), (0, 0)))
    sum_down = Sum(grad_down, more(hidden), place)
    sum_down.given, grad_down = barrier((sum_down.given, grad_down))
    sum_down.over_cores()
    sum_down.over_y()
    grad_gate, grad_up = geglu_pull(dot(down_t, grad_down, ((0,), (0,))))
    grad_gate, grad_up = grad_gate.astype(LOW), grad_up.astype(LOW)
    grad_pair = jnp.concatenate([more(grad_gate), more(grad_up)], axis=0)
    grad_pair, grad_gate, grad_up = barrier((grad_pair, grad_gate, grad_up))
    sum_pair = Sum(ffn_in, grad_pair, place)
    sum_pair.given, grad_gate, grad_up = barrier((sum_pair.given, grad_gate, grad_up))
    sum_pair.over_cores()
    own, far, left, right = row_scatter_parts(
        dot(gate_weight, grad_gate, ((1,), (0,))) + dot(up_weight, grad_up, ((1,), (0,)))
    )
    own, sum_pair.held = barrier((own, sum_pair.held))
    sum_pair.over_y()
    grad_ffn_in = own + left.astype(WIDE) + right.astype(WIDE) + far.astype(WIDE)

    grad_mid_norm, grad_g_pre_ffn = norm_back(middle, ffn_factor, gain_pre_ffn, grad_ffn_in)
    grad_middle = upstream + grad_mid_norm
    grad_branch, grad_g_post_attn = norm_back(branch, post_factor, gain_post_attn, grad_middle)
    grad_branch = row_gather(grad_branch.astype(LOW))
    sum_down.over_col()
    grad_branch, sum_down.total = barrier((grad_branch, sum_down.total))
    sum_down.over_hi()
    grad_mixed = dot(out_weight, grad_branch, ((0,), (0,))).astype(LOW)

    grad_probs = dot(value_all, grad_mixed, ((0,), (0,)))
    grad_value_all = dot(grad_mixed, probs_low, ((1,), (1,)))
    grad_scores = (
        probs * (grad_probs - jnp.sum(probs * grad_probs, axis=0, keepdims=True))
    ).astype(LOW)
    grad_query_rot = dot(key_all, grad_scores, ((1,), (0,)))
    grad_key_all = dot(query_low, grad_scores, ((1,), (1,)))
    grad_kv_all = jnp.concatenate([grad_key_all, grad_value_all], axis=0)
    count = grad_kv_all.shape[1] // 2
    grad_kv_other = to_partner(grad_kv_all[:, count:].astype(LOW))
    grad_kv = grad_kv_all[:, :count] + grad_kv_other.astype(WIDE)
    grad_query, grad_g_query = query_pull(grad_query_rot)
    grad_key, grad_g_key = key_pull(grad_kv[:head])
    grad_query = grad_query.astype(LOW)
    grad_kv = jnp.concatenate([grad_key, grad_kv[head:]], axis=0).astype(LOW)
    grad_qkv = jnp.concatenate([grad_query, grad_kv], axis=0)

    grad_attn_part = dot(qkv_weight, grad_qkv, ((1,), (0,)))
    grad_g_in = jnp.sum(grad_attn_part * attn_in.astype(WIDE), axis=1) / gain_in[:, 0]

    head_gains = jnp.pad(
        jnp.stack([grad_g_query, grad_g_key], axis=1), ((0, features - head), (0, 0))
    )
    head_gains = mix(head_gains, head_gains)
    grad_gains = jnp.concatenate(
        [
            jnp.stack([grad_g_in, grad_g_post_attn, grad_g_pre_ffn, grad_g_post_ffn], axis=1),
            head_gains,
        ],
        axis=1,
    )
    slack = -grad_gains.shape[1] % 128
    gain_columns = jnp.pad(grad_gains, ((0, 0), (0, slack))).astype(LOW)

    def small_part(rows):
        return jnp.concatenate(
            [
                dot(attn_in[rows], grad_query, ((1,), (1,))).astype(LOW),
                dot(grad_branch[rows], mixed, ((1,), (1,))).astype(LOW),
                dot(attn_in[rows], grad_kv, ((1,), (1,))).astype(LOW),
                gain_columns[rows],
            ],
            axis=1,
        )

    sum_small = Small(small_part(slice(features, None)), small_part(slice(features)), place)
    own, *sent = row_chunks(grad_attn_part)
    sum_small.given, sum_pair.total, sum_down.total, *sent = barrier(
        (sum_small.given, sum_pair.total, sum_down.total, *sent)
    )
    sum_small.over_cores()
    sum_pair.over_z()
    own, far, left, right = send_chunks(own, *sent)
    grad_attn_in = own + left.astype(WIDE) + right.astype(WIDE) + far.astype(WIDE)
    sum_small.over_y_directly()
    grad_in_norm, _ = norm_back(x, attn_factor, gain_in, grad_attn_in)
    grad_inputs = (grad_middle + grad_in_norm).astype(LOW)
    sum_small.total, sum_pair.total, grad_inputs = barrier(
        (sum_small.total, sum_pair.total, grad_inputs)
    )
    block_out, grad_inputs = back_together(block_out, grad_inputs)
    shared = Shared([sum_pair, sum_down], place)
    shared.share_y_nearest()
    sum_small.over_z()
    sum_small.total, shared.near = barrier((sum_small.total, shared.near))
    shared.share_y_farthest()
    sum_small.over_row(2 * head)
    sum_small.total, shared.across, block_out, grad_inputs = barrier(
        (sum_small.total, shared.across, block_out, grad_inputs)
    )
    sum_small.share_y()
    grad_w_all = shared.share_cores_last()
    columns = lambda start, count: grad_w_all[:, start : start + count]
    small, grad_w_gate, grad_w_up, grad_w_down = sum_small.share_cores(
        *[columns(i * wide, hidden_share).astype(WIDE) for i in range(3)]
    )
    grad_w_query, grad_w_out = small[:, :head], small[:, head : 2 * head]
    grad_w_key, grad_w_value = small[:, 2 * head : 3 * head], small[:, 3 * head : 4 * head]
    summed = small[:, 4 * head : 4 * head + 6].astype(WIDE).T

    return (
        block_out.T[None],
        grad_inputs.T[None],
        grad_w_query.astype(WIDE),
        grad_w_key.astype(WIDE),
        grad_w_value.astype(WIDE),
        grad_w_out.astype(WIDE).T,
        grad_w_gate,
        grad_w_up,
        grad_w_down.T,
        summed[0],
        summed[4, :head],
        summed[5, :head],
        summed[1],
        summed[2],
        summed[3],
    )


def solution(mesh):
    placed = (
        P("dp", "row", "col"),
        P("col", "row"),
        P("col", None),
        P("col", None),
        P("row", "col"),
        P("col", "row"),
        P("col", "row"),
        P("row", "col"),
        P("col"),
        P(),
        P(),
        P("col"),
        P("col"),
        P("col"),
        P("dp", "row", "col"),
    )
    return jax.shard_map(
        local,
        mesh=mesh,
        in_specs=placed,
        out_specs=(
            P("dp", "row", "col"),
            P("dp", "row", "col"),
            P("col", "row"),
            P("col", None),
            P("col", None),
            P("row", "col"),
            P("col", "row"),
            P("col", "row"),
            P("row", "col"),
            P("col"),
            P(),
            P(),
            P("col"),
            P("col"),
            P("col"),
        ),
        check_vma=False,
    )
```

```python
import jax
import jax.numpy as jnp
import numpy as np
from jax import lax
from jax.experimental import pallas as pl
from jax.experimental.pallas import tpu as pltpu
from jax.sharding import PartitionSpec as P

WINDOW = 512
EPSILON = 1e-06
MASKED = -1e30
ROPE_BASE = 10000.0
LOW = jnp.bfloat16
WIDE = jnp.float32

Y, HI, CORE, COL, ROW = 4, 2, 2, 2, 4


def device(y, z, core):
    return ((y * HI + z // COL) * CORE + core) * COL + z % COL


def z_route(shift_of):
    return [
        (device(y, z, core), device(y, (z + shift_of(z, core)) % 4, core))
        for y in range(Y)
        for z in range(4)
        for core in range(CORE)
    ]


def dp_route(target):
    return [(i, target(i)) for i in range(Y * HI * CORE)]


def by_z(shift_of):
    route = z_route(shift_of)
    return lambda v: lax.ppermute(v, ("dp", "col"), route)


to_partner = by_z(lambda z, core: 1 if z % 2 == 0 else -1)
to_cross = by_z(lambda z, core: -1 if z % 2 == 0 else 1)
to_opposite = by_z(lambda z, core: 2)
z_ring = by_z(lambda z, core: -1 if core == 0 else 1)


def core_swap(v):
    return lax.ppermute(v, "dp", dp_route(lambda i: i ^ 1))


def y_ring(v):
    step = HI * CORE
    return lax.ppermute(
        v, "dp", dp_route(lambda i: (i + (step if i % 2 == 0 else -step)) % (Y * step))
    )


def y_shift(v, distance):
    step = HI * CORE * distance
    return lax.ppermute(v, "dp", dp_route(lambda i: (i + step) % (Y * HI * CORE)))


def row_shift(v, distance):
    return lax.ppermute(v, "row", [(i, (i + distance) % ROW) for i in range(ROW)])


def row_gather(v):
    return jnp.concatenate([v, row_shift(v, 1), row_shift(v, -1), row_shift(v, 2)], axis=1)


def row_chunks(total):
    share = total.shape[1] // ROW
    own, *others = [total[:, i * share : (i + 1) * share] for i in range(ROW)]
    return [own] + [others[i].astype(LOW) for i in (2, 0, 1)]


def send_chunks(own, *sent):
    return [own] + [row_shift(part, distance) for part, distance in zip(sent, (2, -1, 1))]


def row_scatter_parts(total):
    return send_chunks(*row_chunks(total))


def row_scatter(total):
    own, *parts = row_scatter_parts(total)
    for part in parts:
        own = own + part.astype(WIDE)
    return own


def dot(left, right, dims):
    return lax.dot_general(left, right, (dims, ((), ())), preferred_element_type=WIDE)


def norm(v, gain):
    factor = lax.rsqrt(jnp.sum(v * v, axis=0, keepdims=True) / v.shape[0] + EPSILON)
    return v * factor * gain, factor


def norm_back(v, factor, gain, upstream):
    scaled = upstream * gain
    inner = jnp.sum(scaled * v, axis=0, keepdims=True)
    grad = factor * scaled - v * (factor * factor * factor) * inner / v.shape[0]
    return grad, jnp.sum(upstream * v * factor, axis=1)


def head_map(raw, gain, cosine, sine, scaling):
    normed = (
        raw * lax.rsqrt(jnp.mean(raw * raw, axis=0, keepdims=True) + EPSILON) * gain[:, None]
    )
    half = raw.shape[0] // 2
    first, second = normed[:half], normed[half:]
    turned = jnp.concatenate(
        [first * cosine - second * sine, second * cosine + first * sine], axis=0
    )
    return turned * scaling


def geglu(gate, up):
    return jax.nn.gelu(gate, approximate=True) * up


def rope_tables(length, head_size):
    half = head_size // 2
    exponent = np.arange(half, dtype=np.float32) * np.float32(2.0 / head_size)
    rate = np.float32(ROPE_BASE) ** (-exponent)
    angles = rate[:, None] * np.arange(length, dtype=np.float32)[None, :]
    return np.stack([np.cos(angles), np.sin(angles)]).astype(np.float32)


def pick(v, index, axis):
    return lax.dynamic_index_in_dim(v, index, axis, keepdims=False)


def pack_kernel(core, weight, packed):
    packed[...] = weight[...]


def pack(core, weight):
    block = (weight.shape[0] // 2, weight.shape[1])
    return pl.pallas_call(
        pack_kernel,
        grid_spec=pltpu.PrefetchScalarGridSpec(
            num_scalar_prefetch=1,
            grid=(1,),
            in_specs=[pl.BlockSpec(block, lambda i, core: (core[0], 0))],
            out_specs=pl.BlockSpec(block, lambda i, core: (0, 0)),
        ),
        out_shape=jax.ShapeDtypeStruct(block, weight.dtype),
        compiler_params=pltpu.CompilerParams(vmem_limit_bytes=16 * 2**20),
        cost_estimate=pl.CostEstimate(
            flops=0, bytes_accessed=4 * block[0] * block[1], transcendentals=0
        ),
    )(core.reshape(1), weight)


def join_kernel(count, core, *refs):
    owns, mine, theirs, wholes = [refs[i * count : (i + 1) * count] for i in range(4)]
    step = pl.program_id(0)
    for i in range(count):

        @pl.when(step % 2 == 0)
        def _():
            wholes[i][...] = owns[i][...]

        @pl.when(step == 1)
        def _():
            wholes[i][...] = mine[i][...]

        @pl.when(step == 3)
        def _():
            wholes[i][...] = theirs[i][...]


def join(core, owns, mine, theirs):
    count = len(owns)
    block = (owns[0].shape[0] // 2, owns[0].shape[1])
    part = pl.BlockSpec(block, lambda i, core: (0, 0))
    own = pl.BlockSpec(block, lambda i, core: (jnp.where(i < 2, core[0], 1 - core[0]), 0))
    return pl.pallas_call(
        lambda *refs: join_kernel(count, *refs),
        grid_spec=pltpu.PrefetchScalarGridSpec(
            num_scalar_prefetch=1,
            grid=(4,),
            in_specs=[own] * count + [part] * (2 * count),
            out_specs=[pl.BlockSpec(block, lambda i, core: (i, 0))] * count,
        ),
        out_shape=[jax.ShapeDtypeStruct((4 * block[0], block[1]), owns[0].dtype)] * count,
        compiler_params=pltpu.CompilerParams(vmem_limit_bytes=40 * 2**20),
        cost_estimate=pl.CostEstimate(
            flops=0, bytes_accessed=16 * count * block[0] * block[1], transcendentals=0
        ),
    )(core.reshape(1), *owns, *mine, *theirs)


def add(a, b):
    return (a.astype(WIDE) + b.astype(WIDE)).astype(LOW)


Y_GROUPS = [[y * HI * CORE + i for y in range(Y)] for i in range(HI * CORE)]


class Sum:
    def __init__(self, left, right, place):
        self.y, self.z, self.core = place
        rows, self.width = left.shape[0] // 2, right.shape[0]
        product = lambda part: dot(part, right, ((1,), (1,))).astype(LOW)
        self.given, self.kept = product(left[rows:]), product(left[:rows])

    def over_cores(self):
        held = add(self.kept, core_swap(self.given))
        self.held = held.reshape(COL, Y, -1, self.width).swapaxes(0, 1)

    def over_y(self):
        self.total = lax.psum_scatter(
            self.held.reshape(-1, self.width),
            "dp",
            scatter_dimension=0,
            axis_index_groups=Y_GROUPS,
            tiled=True,
        ).reshape(COL, -1, self.width)

    def over_y_directly(self):
        chunk = lambda distance: pick(self.held, (self.y + distance) % Y, 0)
        total = chunk(0).astype(WIDE)
        for distance in (2, 1, 3):
            total = total + y_shift(chunk(distance), distance).astype(WIDE)
        self.total = total.astype(LOW)

    def over_z(self):
        self.over_col()
        self.over_hi()

    def over_col(self):
        self.total = add(self.total[0], to_partner(self.total[1]))

    def over_hi(self):
        self.total = add(self.total, to_opposite(self.total))

    def over_row(self, start):
        sent = self.total[:, start:]
        part = sent.astype(WIDE)
        for distance in (2, 1, 3):
            part = part + row_shift(sent, distance).astype(WIDE)
        self.total = jnp.concatenate([self.total[:, :start], part.astype(LOW)], axis=1)

    def share_y_nearest(self):
        self.near = y_shift(self.total, 1), y_shift(self.total, -1)

    def share_y_farthest(self):
        below, above = self.near
        half = self.width // 2
        self.across = jnp.concatenate(
            [y_shift(below[:, :half], 1), y_shift(above[:, half:], -1)], axis=1
        )
        self.other_near = core_swap(jnp.concatenate([self.total, below, above], axis=0))

    def share_cores_last(self):
        rows = self.total.shape[0]
        below, above = self.near
        other = [self.other_near[i * rows : (i + 1) * rows] for i in range(3)]
        self.lay_y(self.total, below, self.across, above)
        mine = self.mine
        self.lay_y(other[0], other[1], core_swap(self.across), other[2])
        theirs = self.mine
        first = jnp.where(self.core == 0, mine, theirs)
        second = jnp.where(self.core == 0, theirs, mine)
        return jnp.concatenate([first, second], axis=0)

    def share_y(self):
        self.lay_y(self.total, *[y_shift(self.total, distance) for distance in (1, 2, 3)])

    def lay_y(self, *parts):
        ring = jnp.stack(parts)
        self.mine = jnp.concatenate([pick(ring, (self.y - j) % Y, 0) for j in range(Y)], axis=0)

    def share_cores(self, *before):
        theirs = core_swap(self.mine)
        if before:
            theirs, *before = lax.optimization_barrier((theirs, *before))
        first = jnp.where(self.core == 0, self.mine, theirs)
        second = jnp.where(self.core == 0, theirs, self.mine)
        both = jnp.concatenate([first, second], axis=0)
        return (both, *before) if before else both


class Small(Sum):
    def __init__(self, given, kept, place):
        self.y, self.z, self.core = place
        self.given, self.kept, self.width = given, kept, given.shape[1]


class Shared(Sum):
    def __init__(self, sums, place):
        self.y, self.z, self.core = place
        self.total = jnp.concatenate([part.total for part in sums], axis=1)
        self.width = self.total.shape[1]


def local(
    inputs,
    w_query,
    w_key,
    w_value,
    attention_output_weight,
    w_gate,
    w_up,
    down_weight,
    g_in,
    g_query,
    g_key,
    g_post_attn,
    g_pre_ffn,
    g_post_ffn,
    cotangent,
):
    col, row, dp = lax.axis_index("col"), lax.axis_index("row"), lax.axis_index("dp")
    core, hi, y = dp % CORE, (dp // CORE) % HI, dp // (HI * CORE)
    place = (y, hi * COL + col, core)
    features, share = inputs.shape[2], inputs.shape[1] // COL
    head = g_query.shape[0]
    hidden_share = w_gate.shape[1]
    wide = hidden_share + -hidden_share % 256
    barrier = lax.optimization_barrier

    def mix(own, other):
        half = own.shape[0] // 2
        parts = [v[:half] for v in (own, other)], [v[half:] for v in (own, other)]
        first = [jnp.where(core == 0, a, b) for a, b in zip(*parts)]
        second = [jnp.where(core == 0, b, a) for a, b in zip(*parts)]
        return jnp.concatenate(first + second, axis=0)

    def unmix(v):
        half = v.shape[0] // 4
        own_a, other_a, own_b, other_b = [v[i * half : (i + 1) * half] for i in range(4)]
        lay = lambda a, b: jnp.concatenate(
            [jnp.where(core == 0, a, b), jnp.where(core == 0, b, a)], axis=0
        )
        return lay(own_a, own_b), lay(other_a, other_b)

    def spread(v):
        kept = lax.dynamic_slice_in_dim(v, col * share, share, 1)
        given = lax.dynamic_slice_in_dim(v, (1 - col) * share, share, 1)
        return kept, to_partner(given)

    def back_together(*values):
        pairs = [unmix(v) for v in values]
        theirs = to_partner(jnp.concatenate([given for _, given in pairs], axis=0))
        received = [theirs[i * features : (i + 1) * features] for i in range(len(pairs))]
        return [
            jnp.where(
                col == 0,
                jnp.concatenate([kept, other], axis=1),
                jnp.concatenate([other, kept], axis=1),
            )
            for (kept, _), other in zip(pairs, received)
        ]

    kept, taken = spread(inputs[0].T)
    gains_own = jnp.stack([g_in, g_post_attn, g_pre_ffn, g_post_ffn])
    gains_other = to_partner(gains_own)
    gains = mix(gains_own.T, gains_other.T)
    gain_in, gain_post_attn, gain_pre_ffn, gain_post_ffn = [gains[:, i : i + 1] for i in range(4)]

    x = mix(kept, taken).astype(WIDE)
    attn_norm, attn_factor = norm(x, gain_in)
    attn_norm, w_query, w_gate = barrier((attn_norm.astype(LOW), w_query, w_gate))
    attn_in = row_gather(attn_norm)

    attn_own = jnp.concatenate([w_query, w_key, w_value, attention_output_weight.T], axis=1)
    attn_mine = z_ring(pack(core, attn_own))
    gate_mine = z_ring(pack(core, w_gate))
    up_sent, gate_mine = barrier((pack(core, w_up), gate_mine))
    up_mine = z_ring(up_sent)
    (attn_weight,) = join(core, [attn_own], [attn_mine], [core_swap(attn_mine)])
    qkv_weight, out_weight = attn_weight[:, : 3 * head], attn_weight[:, 3 * head :]

    qkv = dot(qkv_weight, attn_in, ((0,), (0,)))
    raw_query, raw_key, value = qkv[:head], qkv[head : 2 * head], qkv[2 * head :].astype(LOW)

    chunk_rows = [row, (row - 1) % ROW, (row + 1) % ROW, (row + 2) % ROW]
    tables = jnp.asarray(rope_tables(ROW * COL * share, head))
    turns = jnp.concatenate(
        [
            lax.dynamic_slice_in_dim(tables, (r * COL + col) * share, share, 2)
            for r in chunk_rows
        ],
        axis=2,
    )
    cosine, sine = turns[0], turns[1]
    query_rot, query_pull = jax.vjp(
        lambda v, g: head_map(v, g, cosine, sine, head**-0.5), raw_query, g_query
    )
    key_rot, key_pull = jax.vjp(lambda v, g: head_map(v, g, cosine, sine, 1.0), raw_key, g_key)
    query_low = query_rot.astype(LOW)
    key_value = jnp.concatenate([key_rot.astype(LOW), value], axis=0)
    key_value_other, down_sent = barrier((to_partner(key_value), pack(core, down_weight.T)))
    down_mine = z_ring(down_sent)
    key_value = jnp.concatenate([key_value, key_value_other], axis=1)
    key_all, value_all = key_value[:head], key_value[head:]

    steps = np.repeat(np.array([0, -1, 1, 2], np.int32), share)
    within = np.tile(np.arange(share, dtype=np.int32), ROW)
    position = lambda c: (((row + steps) % ROW) * COL + c) * share + within
    query_position = position(col)
    key_position = jnp.concatenate([query_position, position(1 - col)])
    offset = query_position[None, :] - key_position[:, None]
    allowed = (offset >= 0) & (offset < WINDOW)
    scores = jnp.where(allowed, dot(key_all, query_low, ((0,), (0,))), MASKED)
    weights = jnp.exp(scores - jnp.max(scores, axis=0, keepdims=True))
    probs = weights / jnp.sum(weights, axis=0, keepdims=True)
    probs_low = probs.astype(LOW)
    mixed = dot(value_all, probs_low, ((1,), (0,))).astype(LOW)
    branch_part = dot(out_weight, mixed, ((1,), (0,)))
    branch = row_scatter(branch_part)
    pair_mine = [gate_mine, up_mine]
    gate_weight, up_weight = join(
        core, [w_gate, w_up], pair_mine, [core_swap(part) for part in pair_mine]
    )
    down_mine, branch = barrier((down_mine, branch))
    (down_t,) = join(core, [down_weight.T], [down_mine], [core_swap(down_mine)])
    post_attn, post_factor = norm(branch, gain_post_attn)
    middle = x + post_attn
    ffn_norm, ffn_factor = norm(middle, gain_pre_ffn)
    ffn_in = row_gather(ffn_norm.astype(LOW))

    gate = dot(gate_weight, ffn_in, ((0,), (0,)))
    up = dot(up_weight, ffn_in, ((0,), (0,)))
    hidden, geglu_pull = jax.vjp(geglu, gate, up)
    hidden = hidden.astype(LOW)
    down_proj = row_scatter(dot(down_t, hidden, ((1,), (0,))))
    post_ffn, post_ffn_factor = norm(down_proj, gain_post_ffn)
    block_out = (middle + post_ffn).astype(LOW)

    kept, taken = spread(cotangent[0].T)
    upstream = mix(kept, taken).astype(WIDE)
    grad_down, grad_g_post_ffn = norm_back(down_proj, post_ffn_factor, gain_post_ffn, upstream)
    grad_down = row_gather(grad_down.astype(LOW))
    more = lambda v: jnp.pad(v, ((0, wide - hidden_share), (0, 0)))
    sum_down = Sum(grad_down, more(hidden), place)
    sum_down.given, grad_down = barrier((sum_down.given, grad_down))
    sum_down.over_cores()
    sum_down.over_y()
    grad_gate, grad_up = geglu_pull(dot(down_t, grad_down, ((0,), (0,))))
    grad_gate, grad_up = grad_gate.astype(LOW), grad_up.astype(LOW)
    grad_pair = jnp.concatenate([more(grad_gate), more(grad_up)], axis=0)
    grad_pair, grad_gate, grad_up = barrier((grad_pair, grad_gate, grad_up))
    sum_pair = Sum(ffn_in, grad_pair, place)
    sum_pair.given, grad_gate, grad_up = barrier((sum_pair.given, grad_gate, grad_up))
    sum_pair.over_cores()
    own, far, left, right = row_scatter_parts(
        dot(gate_weight, grad_gate, ((1,), (0,))) + dot(up_weight, grad_up, ((1,), (0,)))
    )
    own, sum_pair.held = barrier((own, sum_pair.held))
    sum_pair.over_y()
    grad_ffn_in = own + left.astype(WIDE) + right.astype(WIDE) + far.astype(WIDE)

    grad_mid_norm, grad_g_pre_ffn = norm_back(middle, ffn_factor, gain_pre_ffn, grad_ffn_in)
    grad_middle = upstream + grad_mid_norm
    grad_branch, grad_g_post_attn = norm_back(branch, post_factor, gain_post_attn, grad_middle)
    grad_branch = row_gather(grad_branch.astype(LOW))
    sum_down.over_col()
    grad_branch, sum_down.total = barrier((grad_branch, sum_down.total))
    sum_down.over_hi()
    grad_mixed = dot(out_weight, grad_branch, ((0,), (0,))).astype(LOW)

    grad_probs = dot(value_all, grad_mixed, ((0,), (0,)))
    grad_value_all = dot(grad_mixed, probs_low, ((1,), (1,)))
    grad_scores = (
        probs * (grad_probs - jnp.sum(probs * grad_probs, axis=0, keepdims=True))
    ).astype(LOW)
    grad_query_rot = dot(key_all, grad_scores, ((1,), (0,)))
    grad_key_all = dot(query_low, grad_scores, ((1,), (1,)))
    grad_kv_all = jnp.concatenate([grad_key_all, grad_value_all], axis=0)
    count = grad_kv_all.shape[1] // 2
    grad_kv_other = to_partner(grad_kv_all[:, count:].astype(LOW))
    grad_kv = grad_kv_all[:, :count] + grad_kv_other.astype(WIDE)
    grad_query, grad_g_query = query_pull(grad_query_rot)
    grad_key, grad_g_key = key_pull(grad_kv[:head])
    grad_query = grad_query.astype(LOW)
    grad_kv = jnp.concatenate([grad_key, grad_kv[head:]], axis=0).astype(LOW)
    grad_qkv = jnp.concatenate([grad_query, grad_kv], axis=0)

    grad_attn_part = dot(qkv_weight, grad_qkv, ((1,), (0,)))
    grad_g_in = jnp.sum(grad_attn_part * attn_in.astype(WIDE), axis=1) / gain_in[:, 0]

    head_gains = jnp.pad(
        jnp.stack([grad_g_query, grad_g_key], axis=1), ((0, features - head), (0, 0))
    )
    head_gains = mix(head_gains, head_gains)
    grad_gains = jnp.concatenate(
        [
            jnp.stack([grad_g_in, grad_g_post_attn, grad_g_pre_ffn, grad_g_post_ffn], axis=1),
            head_gains,
        ],
        axis=1,
    )
    slack = -grad_gains.shape[1] % 128
    gain_columns = jnp.pad(grad_gains, ((0, 0), (0, slack))).astype(LOW)

    def small_part(rows):
        return jnp.concatenate(
            [
                dot(attn_in[rows], grad_query, ((1,), (1,))).astype(LOW),
                dot(grad_branch[rows], mixed, ((1,), (1,))).astype(LOW),
                dot(attn_in[rows], grad_kv, ((1,), (1,))).astype(LOW),
                gain_columns[rows],
            ],
            axis=1,
        )

    sum_small = Small(small_part(slice(features, None)), small_part(slice(features)), place)
    own, *sent = row_chunks(grad_attn_part)
    sum_small.given, sum_pair.total, sum_down.total, *sent = barrier(
        (sum_small.given, sum_pair.total, sum_down.total, *sent)
    )
    sum_small.over_cores()
    sum_pair.over_z()
    own, far, left, right = send_chunks(own, *sent)
    grad_attn_in = own + left.astype(WIDE) + right.astype(WIDE) + far.astype(WIDE)
    sum_small.over_y_directly()
    sum_small.total, sum_pair.total, grad_attn_in = barrier(
        (sum_small.total, sum_pair.total, grad_attn_in)
    )
    grad_in_norm, _ = norm_back(x, attn_factor, gain_in, grad_attn_in)
    grad_inputs = (grad_middle + grad_in_norm).astype(LOW)
    block_out, grad_inputs = back_together(block_out, grad_inputs)
    shared = Shared([sum_pair, sum_down], place)
    shared.share_y_nearest()
    sum_small.over_z()
    sum_small.total, shared.near = barrier((sum_small.total, shared.near))
    shared.share_y_farthest()
    sum_small.over_row(2 * head)
    sum_small.total, shared.across, block_out, grad_inputs = barrier(
        (sum_small.total, shared.across, block_out, grad_inputs)
    )
    sum_small.share_y()
    grad_w_all = shared.share_cores_last()
    columns = lambda start, count: grad_w_all[:, start : start + count]
    small, grad_w_gate, grad_w_up, grad_w_down = sum_small.share_cores(
        *[columns(i * wide, hidden_share).astype(WIDE) for i in range(3)]
    )
    grad_w_query, grad_w_out = small[:, :head], small[:, head : 2 * head]
    grad_w_key, grad_w_value = small[:, 2 * head : 3 * head], small[:, 3 * head : 4 * head]
    summed = small[:, 4 * head : 4 * head + 6].astype(WIDE).T

    return (
        block_out.T[None],
        grad_inputs.T[None],
        grad_w_query.astype(WIDE),
        grad_w_key.astype(WIDE),
        grad_w_value.astype(WIDE),
        grad_w_out.astype(WIDE).T,
        grad_w_gate,
        grad_w_up,
        grad_w_down.T,
        summed[0],
        summed[4, :head],
        summed[5, :head],
        summed[1],
        summed[2],
        summed[3],
    )


def solution(mesh):
    placed = (
        P("dp", "row", "col"),
        P("col", "row"),
        P("col", None),
        P("col", None),
        P("row", "col"),
        P("col", "row"),
        P("col", "row"),
        P("row", "col"),
        P("col"),
        P(),
        P(),
        P("col"),
        P("col"),
        P("col"),
        P("dp", "row", "col"),
    )
    return jax.shard_map(
        local,
        mesh=mesh,
        in_specs=placed,
        out_specs=(
            P("dp", "row", "col"),
            P("dp", "row", "col"),
            P("col", "row"),
            P("col", None),
            P("col", None),
            P("row", "col"),
            P("col", "row"),
            P("col", "row"),
            P("row", "col"),
            P("col"),
            P(),
            P(),
            P("col"),
            P("col"),
            P("col"),
        ),
        check_vma=False,
    )
```
